32 devices in a mesh: sec: 2 (over core), tile: 16 (over z, y, x).
Axes of the slice: x: 2, y: 2, z: 4, core: 2. Of those that a mesh axis runs over, the one named last changes fastest.
Arguments:
- land_wind: float32 [4096, 128], P(('sec', 'tile')), may hold values from 0.15 to 0.9
- land_moist: float32 [4096, 128], P(('sec', 'tile')), may hold values from 0 to 0.3
- texture: int32 [4096, 128], P(('sec', 'tile')), may hold values from 0 to 3
- land_index: int32 [4096, 128], P(('sec', 'tile')), may hold values from 0 to 32767
- erod_map: float32 [1048576], P(('sec', 'tile')), may hold values from 0.2 to 1
- mass_frac: float32 [4, 12], replicated, may hold values from 0.02 to 0.3
- blast_table: float32 [4, 8, 12], replicated, may hold values from 0.05 to 1
- dest_tile: int32 [4096, 1], P(('sec', 'tile')), may hold values from 0 to 31; in each aligned block of 128 rows (0 to 127, 128 to 255, ...) at most 8 rows name the same one
- regrid_w: bfloat16 [4096, 128, 256], P(('sec', 'tile')), may hold values from 0 to 0.25, as said below
- atm_state: float32 [3, 16, 8192], P(None, None, ('sec', 'tile')), may hold values from -5 to 5
- dust_mix: float32 [8, 16, 8192], P(None, None, ('sec', 'tile')), may hold values from 0 to 1
- mixing: float32 [15, 8192], P(None, ('sec', 'tile')), may hold values from 0.1 to 10
- settle: float32 [8], replicated, may hold values from 0.05 to 0.5
Outputs:
- land_fields: float32 [2, 4096, 128], P(None, ('sec', 'tile'))
- dust_out: float32 [8, 16, 8192], P(None, None, ('sec', 'tile'))
The draws below stay inside these ranges and needn't reach their ends.
Inputs may be any that keep to these rules, and one draw needn't show every extreme that they name: `land_index`: each land cell's index points into its own device's 32768 cells of erod_map. `dest_tile`: among the 128 blocks of one device at most 8 name the same tile, a bound that some block reaches. `regrid_w`: each land cell has 1 to 4 positive weights, of 0.05 or more, on adjacent columns of its tile, and 0 elsewhere.
All inputs are finite; a program needn't handle non-finite values.
Results may differ from the reference program's by a relative error of at most 0.0023.
Values may be sent and summed in bfloat16 or wider, within the bound.
A program may use at most 64 MiB of HBM per device.

```python
import math
import jax
import jax.numpy as jnp
import numpy as np
from jax import lax

BINS = 12
DBINS = 8
TEXTURES = 4
BL = 128
LEV = 16
NBLK_DEV = 128
AC = 256
CAP = 8
NB = 4096
COLS = 8192
GRID_DEV = 32768
GRID = 1048576
DEVICES = 32


def draw_regrid_w(key, part):
    key_jitter = jax.random.fold_in(key, 11)
    key_count = jax.random.fold_in(key, 12)
    key_value = jax.random.fold_in(key, 13)
    cells = jnp.arange(BL).astype(jnp.int32)
    base = cells * (AC - 4) // BL
    jitter = jax.random.randint(key_jitter, (NB, BL), 0, 2).astype(jnp.int32)
    first = jnp.minimum(base[None, :] + jitter, AC - 4)
    count = jax.random.randint(key_count, (NB, BL), 1, 5).astype(jnp.int32)
    column = jnp.arange(AC).astype(jnp.int32)
    inside = (column[None, None, :] >= first[:, :, None]) & (column[None, None, :] < first[:, :, None] + count[:, :, None])
    values = jax.random.uniform(key_value, (NB, BL, AC), jnp.float32, 0.1, 0.25)
    return jnp.where(inside, values, jnp.float32(0.0)).astype(jnp.bfloat16)


def set_ends(values, rng, least, largest):
    longest = values.shape.index(max(values.shape))
    spots = []
    for shift in (0, 1):
        where = [jax.random.randint(jax.random.fold_in(rng, axis), (), 0, length) for axis, length in enumerate(values.shape)]
        where[longest] = (where[longest] + shift) % values.shape[longest]
        spots.append(tuple(where))
    return values.at[spots[0]].set(least).at[spots[1]].set(largest)


def shard_levels(own_key, shape, split, smallest, top_value):
    def one(axis_at, parts):
        draws = jax.random.uniform(jax.random.fold_in(jax.random.fold_in(own_key, 6), axis_at), (parts,), jnp.float32, smallest / len(split), top_value / len(split))
        return jnp.repeat(jnp.exp(draws), shape[axis_at] // parts).reshape((-1,) + (1,) * (len(shape) - axis_at - 1))

    loudness = one(*split[0])
    for cut in split[1:]:
        loudness = loudness * one(*cut)
    return loudness


def assign_block(key, own, number, rows, amount, top, reach, lean):
    sequence = jax.random.permutation(key, amount)
    heavy_load, common = portions_of(amount, rows * top, reach, lean, True), portions_of(amount, rows * top, reach, lean, False)
    places = jnp.arange(amount)

    def named(tallies, turn):
        used = int((tallies > 0).sum())
        fixed = max(1, used // 4)
        shifted = fixed + (places - fixed + turn * (used - fixed)) % max(1, amount - fixed)
        return jnp.zeros((amount,), jnp.int32).at[sequence[jnp.where(places < fixed, places, shifted)]].set(jnp.asarray(tallies, jnp.int32))

    tallies = jnp.where(number % 4 == 0, named(heavy_load, number // 4), named(common, number - number // 4 - 1))
    mixed = jax.random.permutation(jax.random.fold_in(own, 3), amount)
    donor, receiver = mixed[0:amount // 2 * 2:2], mixed[1:amount // 2 * 2:2]
    margin = jnp.minimum(tallies[donor] - 1, reach - tallies[receiver]) // 2
    margin = jnp.where((donor == sequence[0]) | (receiver == sequence[0]) | (tallies[receiver] == 0), 0, jnp.maximum(margin, 0))
    shifted = jax.random.randint(jax.random.fold_in(own, 4), (amount // 2,), 0, 1 << 20) % (margin + 1)
    tallies = tallies.at[donor].add(-shifted).at[receiver].add(shifted)
    items = jnp.searchsorted(jnp.cumsum(tallies), jnp.arange(rows * top), side="right").astype(jnp.int32)
    grid = items.reshape(top, rows).T
    grid = grid[jax.random.permutation(jax.random.fold_in(own, 1), rows)]
    turn = jax.random.randint(jax.random.fold_in(own, 2), (rows, 1), 0, top)
    return jnp.take_along_axis(grid, (jnp.arange(top)[None, :] + turn) % top, axis=1)


def portions_of(amount, total, reach, lean, full):
    weights = [(1 << 20) // math.isqrt(rank ** lean) + 1 for rank in range(1, amount + 1)]
    largest = reach if full else min(reach, max(-(-total // amount), total * weights[0] // sum(weights)))
    least = 1 if total - largest >= amount - 1 else 0
    counts, surplus = [largest] + [least] * (amount - 1), total - largest - least * (amount - 1)
    while surplus > 0:
        movable = [i for i in range(1, amount) if counts[i] < largest] or [i for i in range(1, amount) if counts[i] < reach]
        mass, left = sum([weights[i] for i in movable]), surplus
        for i in movable:
            more = min(reach - counts[i], max(1, left * weights[i] // mass), surplus)
            counts[i] = counts[i] + more
            surplus = surplus - more
    return np.array(counts)


def centred(key, shape, width, most, pieces=(), held_as=jnp.bfloat16):
    entries = width * jax.random.normal(key, shape, jnp.float32)
    if pieces:
        entries = entries * shard_levels(key, shape, pieces, -0.22, 0.18)
    return jnp.clip(entries, -most, most).astype(held_as)


def setup_inputs(seed: int = 0) -> dict:
    key_of = jax.random.split(jax.random.key(seed), 14)
    land_wind = jnp.clip(jnp.exp(math.log(0.9) - 1.7917594 * jax.random.uniform(key_of[0], (NB, BL), jnp.float32) ** shard_levels(key_of[0], (NB, BL), ((0, 32),), -0.2, 0.2)), 0.15, 0.9)
    land_moist = jnp.clip(0.3 * jax.random.uniform(key_of[1], (NB, BL), jnp.float32) ** shard_levels(key_of[1], (NB, BL), ((0, 32),), -0.2, 0.2), 0.0, 0.3)
    texture = set_ends(jax.random.randint(key_of[2], (NB, BL), 0, TEXTURES), jax.random.fold_in(key_of[2], 1), 0, TEXTURES - 1).astype(jnp.int32)
    land_index = set_ends(jax.random.randint(key_of[3], (NB, BL), 0, GRID_DEV), jax.random.fold_in(key_of[3], 1), 0, GRID_DEV - 1).astype(jnp.int32)
    erod_map = jnp.clip(0.2 + 0.8 * jax.random.uniform(key_of[4], (GRID,), jnp.float32) ** shard_levels(key_of[4], (GRID,), ((0, 32),), -0.2, 0.2), 0.2, 1.0)
    mass_frac = jnp.clip(jnp.exp(jax.random.uniform(key_of[5], (TEXTURES, BINS), jnp.float32, math.log(0.02), math.log(0.3))), 0.02, 0.3)
    blast_table = jnp.clip(jnp.exp(jax.random.uniform(key_of[6], (TEXTURES, DBINS, BINS), jnp.float32, math.log(0.05), math.log(1.0))), 0.05, 1.0)
    dest_tile_keys = jax.random.split(jax.random.fold_in(key_of[7], 1), NB // NBLK_DEV)
    dest_tile_turns = jax.random.permutation(jax.random.fold_in(key_of[7], 3), NB // NBLK_DEV)
    dest_tile = jax.vmap(lambda own, number: assign_block(jax.random.fold_in(key_of[7], 2), own, number, NBLK_DEV, DEVICES, 1, CAP, 2))(dest_tile_keys, dest_tile_turns).reshape((NB, 1))
    regrid_w = draw_regrid_w(jax.random.fold_in(key_of[13], 71), 0)
    atm_state = centred(key_of[9], (3, LEV, COLS), 1.0, 5.0, ((2, 32),), jnp.float32)
    dust_mix = jnp.clip(1.0 * jax.random.uniform(key_of[10], (DBINS, LEV, COLS), jnp.float32) ** shard_levels(key_of[10], (DBINS, LEV, COLS), ((2, 32),), -0.2, 0.2), 0.0, 1.0)
    mixing = jnp.clip(jnp.exp(math.log(10.0) - 4.6051702 * jax.random.uniform(key_of[11], (LEV - 1, COLS), jnp.float32) ** shard_levels(key_of[11], (LEV - 1, COLS), ((1, 32),), -0.2, 0.2)), 0.1, 10.0)
    settle = jnp.clip(jax.random.uniform(key_of[12], (DBINS,), jnp.float32, 0.05, 0.5), 0.05, 0.5)
    return {"land_wind": land_wind, "land_moist": land_moist, "texture": texture, "land_index": land_index, "erod_map": erod_map, "mass_frac": mass_frac, "blast_table": blast_table, "dest_tile": dest_tile, "regrid_w": regrid_w, "atm_state": atm_state, "dust_mix": dust_mix, "mixing": mixing, "settle": settle}


def threshold_table(count):
    diameter = 4e-05 * jnp.power(jnp.float32(1.35), jnp.arange(count).astype(jnp.float32))
    return jnp.sqrt(0.0123 * (2160.0 * 9.81 * diameter + 0.0003 / (1.227 * diameter)))

def emit(wind_rows, moist_rows, texture_rows, erodible, mass_frac, blast_table, base_thresh):
    high = lax.Precision.HIGHEST
    thresh = base_thresh[:, None, None] * jnp.sqrt(1.0 + 12.1 * moist_rows)[None]
    classes = jnp.arange(mass_frac.shape[0]).astype(jnp.int32)
    onehot = (texture_rows[None] == classes[:, None, None]).astype(jnp.float32)
    fraction = jnp.einsum('tb,tnl->bnl', mass_frac, onehot, precision=high)
    speed = wind_rows[None]
    salt = 40.0 * fraction * erodible[None] * (speed + thresh) * jnp.maximum(speed * speed - thresh * thresh, 0.0)
    blasted = jnp.einsum('tkb,bnl->tknl', blast_table, salt, precision=high)
    emission = lax.optimization_barrier(jnp.sum(blasted * onehot[:, None], axis=0))
    return jnp.transpose(emission, (1, 0, 2)).astype(jnp.bfloat16)

def solve(right_side, coupling, sinking):
    levels = right_side.shape[1]
    sink_col = sinking[:, None]
    zero_row = jnp.zeros_like(coupling[0])
    ratios = []
    partial_value = []
    ratio_prev = None
    part_prev = None
    for level in range(levels):
        lower_c = coupling[level - 1] if level > 0 else zero_row
        upper_c = coupling[level] if level < levels - 1 else zero_row
        diagonal = 1.0 + lower_c[None] + upper_c[None] + sink_col
        if level == 0:
            pivot = diagonal
            part_now = right_side[:, level] / pivot
        else:
            pivot = diagonal + lower_c[None] * ratio_prev
            part_now = (right_side[:, level] + lower_c[None] * part_prev) / pivot
        if level < levels - 1:
            ratio_now = -(upper_c[None] + sink_col) / pivot
        else:
            ratio_now = jnp.zeros_like(pivot)
        ratios.append(ratio_now)
        partial_value.append(part_now)
        ratio_prev = ratio_now
        part_prev = part_now
    result = [None] * levels
    result[levels - 1] = partial_value[levels - 1]
    for level in range(levels - 2, -1, -1):
        result[level] = partial_value[level] - ratios[level] * result[level + 1]
    return jnp.stack(result, axis=1)

def reference(land_wind, land_moist, texture, land_index, erod_map, mass_frac, blast_table, dest_tile, regrid_w, atm_state, dust_mix, mixing, settle):
    high = lax.Precision.HIGHEST
    base_thresh = threshold_table(mass_frac.shape[1])
    items = (land_wind.reshape(DEVICES, NBLK_DEV, BL), land_moist.reshape(DEVICES, NBLK_DEV, BL), texture.reshape(DEVICES, NBLK_DEV, BL), land_index.reshape(DEVICES, NBLK_DEV, BL), erod_map.reshape(DEVICES, GRID_DEV), dest_tile.reshape(DEVICES, NBLK_DEV), regrid_w.reshape(DEVICES, NBLK_DEV, BL, AC))

    def forward(total, item):
        wind_rows, moist_rows, texture_rows, index_rows, soil_map, targets, weights = item
        erodible = soil_map[index_rows]
        emission = emit(wind_rows, moist_rows, texture_rows, erodible, mass_frac, blast_table, base_thresh)
        partial_flux = jnp.einsum('gkl,gla->gka', emission.astype(jnp.float32), weights.astype(jnp.float32), precision=high)
        return (total + jax.ops.segment_sum(partial_flux, targets, num_segments=DEVICES), None)
    start = jnp.zeros((DEVICES, DBINS, AC), jnp.float32)
    summed, _ = lax.scan(forward, start, items)
    flux = jnp.transpose(summed * (float(AC) / float(BL * NBLK_DEV)), (1, 0, 2)).reshape(DBINS, COLS)
    state = solve(atm_state, mixing, jnp.zeros((3,), jnp.float32))
    speed = jnp.sqrt(state[0, 0] ** 2 + state[1, 0] ** 2 + 0.25)
    surface = jnp.stack([speed, state[2, 0]]).astype(jnp.bfloat16)
    by_tile = jnp.transpose(surface.reshape(2, DEVICES, AC), (1, 0, 2))

    def backward(item):
        moist_rows, targets, weights = item
        picked = by_tile[targets]
        weights_wide = weights.astype(jnp.float32)
        numer = jnp.einsum('gla,gka->kgl', weights_wide, picked.astype(jnp.float32), precision=high)
        denom = lax.optimization_barrier(jnp.sum(weights_wide, axis=2))
        return jnp.stack([numer[0] / denom, 0.5 * moist_rows + 0.5 * numer[1] / denom])
    back = lax.map(backward, (items[1], items[5], items[6]))
    land_fields = jnp.transpose(back, (1, 0, 2, 3)).reshape(2, NB, BL)
    loaded = dust_mix.at[:, 0, :].add(flux)
    dust_out = solve(loaded, mixing, settle)
    return (land_fields, dust_out)
```

```python
import functools

import jax
import jax.numpy as jnp
import numpy as np
from jax import lax
from jax.experimental import pallas as pl
from jax.experimental.pallas import tpu as pltpu
from jax.sharding import PartitionSpec as P

MESH = pl.DeviceIdType.MESH
F32 = jnp.float32
BF16 = jnp.bfloat16
FIXED = 65535.0


def threshold_constants(count):
    diameter = 4e-05 * np.power(1.35, np.arange(count))
    return np.sqrt(0.0123 * (2160.0 * 9.81 * diameter + 0.0003 / (1.227 * diameter)))


def rows_of(values, shape):
    row = lax.broadcasted_iota(jnp.int32, shape, 0)
    total = jnp.zeros(shape, F32)
    for r, value in enumerate(values):
        total = jnp.where(row == r, value, total)
    return total


def kernel(
    n, nt, nblocks, ncells, columns, nbins, nsalt, ntex, levels,
    wind_hbm, moist_hbm, tex_hbm, index_hbm, map_hbm, frac_hbm, blast_hbm, dest_hbm,
    w_hbm, atm_hbm, dust_hbm, mix_hbm, settle_hbm,
    land_out, dust_out,
    wind, moist, tex, index, soil, frac, blast, dest_v, dest_s, w, atm, dust, mix, settle,
    packed, erod, root, coef, part, sums, send, came, mine, gath, numer, base, gain,
    in_sem, w_sem, surf_send, surf_recv, flux_send, flux_recv,
):
    half = columns // 2
    me = lax.axis_index("sec") * nt + lax.axis_index("tile")

    def local(src, dst, k):
        copy = pltpu.make_async_copy(src, dst, in_sem.at[k])
        copy.start()
        return copy

    c_mix = local(mix_hbm, mix, 0)
    c_atm = local(atm_hbm, atm, 1)
    c_map = local(map_hbm, soil, 2)
    c_index = local(index_hbm, index, 3)
    c_wind = local(wind_hbm, wind, 4)
    c_moist = local(moist_hbm, moist, 5)
    c_tex = local(tex_hbm, tex, 6)
    c_frac = local(frac_hbm, frac, 7)
    c_blast = local(blast_hbm, blast, 8)
    c_dv = local(dest_hbm, dest_v, 9)
    c_ds = local(dest_hbm, dest_s, 10)
    c_settle = local(settle_hbm, settle, 11)
    c_d0 = local(dust_hbm.at[:, 0:half], dust.at[0], 12)
    c_d1 = local(dust_hbm.at[:, half:columns], dust.at[1], 13)
    groups = nblocks // 8

    def chunk(i):
        at = pl.ds(i * 8, 8)
        return pltpu.make_async_copy(w_hbm.at[at], w.at[at], w_sem.at[i])

    def fetch(i, carry):
        chunk(i).start()
        return carry

    lax.fori_loop(0, groups, fetch, 0)

    def peer(i):
        p = lax.rem(me + i, n)
        return p, (p // nt, lax.rem(p, nt))

    barrier = pltpu.get_barrier_semaphore()

    def greet(i, carry):
        pl.semaphore_signal(barrier, inc=1, device_id=peer(i)[1], device_id_type=MESH)
        return carry

    lax.fori_loop(1, n, greet, 0)

    c_mix.wait()
    c_atm.wait()
    above = None
    held = [None] * 3
    for level in range(levels - 1, -1, -1):
        pivot = jnp.ones((1, columns), F32)
        low = up = None
        if level > 0:
            low = mix[level - 1:level, :]
            pivot = pivot + low
        if level < levels - 1:
            up = mix[level:level + 1, :]
            pivot = pivot + up * (1.0 - above)
        inverse = 1.0 / pivot
        for f in range(3):
            right = atm[f, level:level + 1, :]
            if up is not None:
                right = right + up * held[f]
            held[f] = right * inverse
        if low is not None:
            above = low * inverse
    speed = jnp.sqrt(held[0] * held[0] + held[1] * held[1] + 0.25)
    mine[0:1, :] = speed.astype(BF16).astype(F32)
    mine[1:2, :] = held[2].astype(BF16).astype(F32)

    c_map.wait()
    c_index.wait()
    words = soil.shape[0] // 2
    fixed = jnp.floor(soil[...] * FIXED + 0.5).astype(jnp.int32)
    packed[...] = fixed[:words] + (fixed[words:] << 16)
    bits = words.bit_length() - 1

    def erode(i, carry):
        at = pl.ds(pl.multiple_of(i * 8, 8), 8)
        cell = index[at, :]
        lane = cell & 127
        row = cell >> 7
        picks = [((row >> b) & 1) == 1 for b in range(bits)]

        def tree(bit, first):
            if bit < 0:
                words_row = jnp.broadcast_to(packed[first:first + 1, :], (8, 128))
                return jnp.take_along_axis(words_row, lane, axis=1, mode="promise_in_bounds")
            return jnp.where(picks[bit], tree(bit - 1, first + (1 << bit)), tree(bit - 1, first))

        word = tree(bits - 1, 0)
        value = jnp.where(row >= words, lax.shift_right_logical(word, 16), word) & 65535
        erod[at, :] = value.astype(F32) * (1.0 / FIXED)
        return carry

    lax.fori_loop(0, groups, erode, 0)

    pl.semaphore_wait(barrier, n - 1)

    def send_surface(i, carry):
        pltpu.make_async_remote_copy(
            src_ref=mine, dst_ref=gath.at[me], send_sem=surf_send, recv_sem=surf_recv,
            device_id=peer(i)[1], device_id_type=MESH,
        ).start()
        return carry

    lax.fori_loop(1, n, send_surface, 0)
    gath[me] = mine[...]

    c_frac.wait()
    c_blast.wait()
    coef[...] = jnp.zeros_like(coef)
    for t in range(ntex):
        coef[:, 16 * t:16 * t + nsalt] = 40.0 * blast[t] * frac[t:t + 1, :]
    full = coef[:, 0:16 * ntex]
    coarse = full.astype(BF16)
    fine = (full - coarse.astype(F32)).astype(BF16)
    table = jnp.concatenate([coarse, fine], axis=0)
    c_wind.wait()
    c_moist.wait()
    c_tex.wait()
    root[...] = jnp.sqrt(1.0 + 12.1 * moist[...])
    thresh0 = rows_of([float(v) for v in threshold_constants(nsalt)], (16, ncells))
    nothing = jnp.zeros((nbins, ncells), F32)

    def regrid(i, carry):
        chunk(i).wait()
        blocks = []
        for j in range(8):
            at = pl.ds(i * 8 + j, 1)
            speed_row = jnp.broadcast_to(wind[at, :], (16, ncells))
            thresh = thresh0 * jnp.broadcast_to(root[at, :], (16, ncells))
            total = speed_row + thresh
            salt = jnp.broadcast_to(erod[at, :], (16, ncells)) * total * (
                total * jnp.maximum(speed_row - thresh, 0.0)
            )
            kind = jnp.broadcast_to(tex[at, :], (16, ncells))
            blocks.append(
                jnp.concatenate(
                    [jnp.where(kind == t, salt, 0.0).astype(BF16) for t in range(ntex)], axis=0
                )
            )
        both = jnp.dot(table, jnp.concatenate(blocks, axis=1), preferred_element_type=F32)
        emission = both[0:nbins] + both[nbins:2 * nbins]
        for j in range(0, 8, 2):
            first = emission[:, j * ncells:(j + 1) * ncells]
            second = emission[:, (j + 1) * ncells:(j + 2) * ncells]
            left = jnp.concatenate(
                [
                    jnp.concatenate([first, nothing], axis=1),
                    jnp.concatenate([nothing, second], axis=1),
                ],
                axis=0,
            ).astype(BF16)
            weights = w[pl.ds(i * 8 + j, 2)].reshape(2 * ncells, columns)
            flux = jnp.dot(left, weights, preferred_element_type=F32)
            for s in range(2):
                at = pl.ds(i * 8 + j + s, nbins, stride=nblocks)
                part[0, at, :] = flux[s * nbins:(s + 1) * nbins, 0:half]
                part[1, at, :] = flux[s * nbins:(s + 1) * nbins, half:columns]
        return carry

    lax.fori_loop(0, groups, regrid, 0)

    c_dv.wait()
    tiles = lax.broadcasted_iota(jnp.int32, (n, nblocks), 0)
    placing = jnp.where(jnp.broadcast_to(dest_v[...], (n, nblocks)) == tiles, 1.0, 0.0).astype(BF16)
    placing = jnp.concatenate([placing, placing], axis=1)
    for k in range(nbins):
        at = slice(k * nblocks, (k + 1) * nblocks)
        block = jnp.concatenate([part[0, at, :], part[1, at, :]], axis=1)
        high = block.astype(BF16)
        low = (block - high.astype(F32)).astype(BF16)
        total = jnp.dot(placing, jnp.concatenate([high, low], axis=0), preferred_element_type=F32)
        sums[pl.ds(k, n, stride=2 * nbins), :] = total[:, 0:half]
        sums[pl.ds(nbins + k, n, stride=2 * nbins), :] = total[:, half:columns]
    send[...] = sums[...].reshape(n, 2 * nbins, half).astype(BF16)

    def send_flux(i, carry):
        p, target = peer(i)
        pltpu.make_async_remote_copy(
            src_ref=send.at[p], dst_ref=came.at[me], send_sem=flux_send, recv_sem=flux_recv,
            device_id=target, device_id_type=MESH,
        ).start()
        return carry

    lax.fori_loop(1, n, send_flux, 0)
    came[me] = send[me]

    c_settle.wait()
    c_d0.wait()
    c_d1.wait()
    sink = rows_of([settle[0, f] for f in range(nbins)], (nbins, columns))
    ratios = [None] * levels
    values = [None] * levels
    for level in range(levels - 1, -1, -1):
        pivot = jnp.ones((nbins, columns), F32)
        at = pl.ds(level, nbins, stride=levels)
        right = jnp.concatenate([dust[0, at, :], dust[1, at, :]], axis=1)
        low = None
        if level > 0:
            low = jnp.broadcast_to(mix[level - 1:level, :], (nbins, columns))
            pivot = pivot + low
        if level < levels - 1:
            up = jnp.broadcast_to(mix[level:level + 1, :], (nbins, columns)) + sink
            pivot = pivot + up * (1.0 - ratios[level + 1])
            right = right + up * values[level + 1]
        else:
            pivot = pivot + sink
        inverse = 1.0 / pivot
        values[level] = right * inverse
        if low is not None:
            ratios[level] = low * inverse
    scale = float(columns) / float(ncells * nblocks)
    now, step = values[0], inverse * scale
    base[0], gain[0] = now, step
    for level in range(1, levels):
        now = values[level] + ratios[level] * now
        step = ratios[level] * step
        base[level], gain[level] = now, step

    c_ds.wait()
    arrived = gath.at[pl.ds(0, n - 1)]
    pltpu.make_async_copy(arrived, arrived, surf_recv).wait()
    rest = jnp.where(lax.broadcasted_iota(jnp.int32, (6, columns), 0) == 0, 1.0, 0.0)

    def back(i, carry):
        for j in range(0, 8, 2):
            g = i * 8 + j
            left = jnp.concatenate(
                [gath[dest_s[0, g]], rest, gath[dest_s[0, g + 1]], rest], axis=0
            ).astype(BF16)
            weights = w[pl.ds(g, 2)].reshape(2 * ncells, columns)
            found = lax.dot_general(
                left, weights, (((1,), (1,)), ((), ())), preferred_element_type=F32
            )
            numer[pl.ds(pl.multiple_of(g * 8, 8), 8), :] = found[0:8, 0:ncells]
            numer[pl.ds(pl.multiple_of(g * 8 + 8, 8), 8), :] = found[8:16, ncells:2 * ncells]
        return carry

    lax.fori_loop(0, groups, back, 0)
    weight = 1.0 / numer[pl.ds(2, nblocks, stride=8), :]
    land_out[0] = numer[pl.ds(0, nblocks, stride=8), :] * weight
    land_out[1] = 0.5 * moist[...] + 0.5 * (numer[pl.ds(1, nblocks, stride=8), :] * weight)

    landed = came.at[pl.ds(0, n - 1)]
    pltpu.make_async_copy(landed, landed, flux_recv).wait()
    flux = jnp.sum(came[...].astype(F32), axis=0)
    flux = jnp.concatenate([flux[0:nbins], flux[nbins:2 * nbins]], axis=1)
    for level in range(levels):
        dust_out[:, level, :] = base[level] + gain[level] * flux

    sent = gath.at[pl.ds(0, n - 1)]
    pltpu.make_async_copy(sent, sent, surf_send).wait()
    gone = came.at[pl.ds(0, n - 1)]
    pltpu.make_async_copy(gone, gone, flux_send).wait()


def on_device(
    nt, land_wind, land_moist, texture, land_index, erod_map, mass_frac, blast_table, dest_tile,
    regrid_w, atm_state, dust_mix, mixing, settle,
):
    nblocks, ncells = land_wind.shape
    columns = regrid_w.shape[2]
    ntex, nbins, nsalt = blast_table.shape
    levels = atm_state.shape[1]
    half = columns // 2
    n = lax.axis_size(("sec", "tile"))
    groups = nblocks // 8
    soil = erod_map.reshape(-1, 128)
    land = pltpu.VMEM((nblocks, ncells), F32)
    whole = pltpu.VMEM((nblocks, ncells), jnp.int32)
    return pl.pallas_call(
        functools.partial(kernel, n, nt, nblocks, ncells, columns, nbins, nsalt, ntex, levels),
        out_shape=(
            jax.ShapeDtypeStruct((2, nblocks, ncells), F32),
            jax.ShapeDtypeStruct((nbins, levels, columns), F32),
        ),
        in_specs=[pl.BlockSpec(memory_space=pl.ANY)] * 13,
        out_specs=(pl.BlockSpec(memory_space=pltpu.VMEM), pl.BlockSpec(memory_space=pltpu.VMEM)),
        scratch_shapes=[
            land,
            land,
            whole,
            whole,
            pltpu.VMEM(soil.shape, F32),
            pltpu.VMEM(mass_frac.shape, F32),
            pltpu.VMEM(blast_table.shape, F32),
            pltpu.VMEM((1, nblocks), jnp.int32),
            pltpu.SMEM((1, nblocks), jnp.int32),
            pltpu.VMEM(regrid_w.shape, BF16),
            pltpu.VMEM(atm_state.shape, F32),
            pltpu.VMEM((2, nbins * levels, half), F32),
            pltpu.VMEM(mixing.shape, F32),
            pltpu.SMEM((1, nbins), F32),
            pltpu.VMEM((soil.shape[0] // 2, 128), jnp.int32),
            land,
            land,
            pltpu.VMEM((nbins, 128), F32),
            pltpu.VMEM((2, nbins * nblocks, half), F32),
            pltpu.VMEM((n * 2 * nbins, half), F32),
            pltpu.VMEM((n, 2 * nbins, half), BF16),
            pltpu.VMEM((n, 2 * nbins, half), BF16),
            pltpu.VMEM((2, columns), F32),
            pltpu.VMEM((n, 2, columns), F32),
            pltpu.VMEM((nblocks * 8, ncells), F32),
            pltpu.VMEM((levels, nbins, columns), F32),
            pltpu.VMEM((levels, nbins, columns), F32),
            pltpu.SemaphoreType.DMA((14,)),
            pltpu.SemaphoreType.DMA((groups,)),
            pltpu.SemaphoreType.DMA,
            pltpu.SemaphoreType.DMA,
            pltpu.SemaphoreType.DMA,
            pltpu.SemaphoreType.DMA,
        ],
        compiler_params=pltpu.CompilerParams(
            collective_id=0, has_side_effects=True, vmem_limit_bytes=40 * 1024 * 1024
        ),
    )(
        land_wind, land_moist, texture, land_index, soil, mass_frac, blast_table,
        dest_tile.reshape(1, nblocks), regrid_w, atm_state,
        dust_mix.reshape(nbins * levels, columns), mixing, settle.reshape(1, nbins),
    )


def solution(mesh):
    both = ("sec", "tile")
    in_specs = (
        P(both, None),
        P(both, None),
        P(both, None),
        P(both, None),
        P(both),
        P(),
        P(),
        P(both, None),
        P(both, None, None),
        P(None, None, both),
        P(None, None, both),
        P(None, both),
        P(),
    )
    out_specs = (P(None, both, None), P(None, None, both))
    return jax.shard_map(
        functools.partial(on_device, mesh.shape["tile"]),
        mesh=mesh, in_specs=in_specs, out_specs=out_specs, check_vma=False,
    )
```

```python
import functools

import jax
import jax.numpy as jnp
import numpy as np
from jax import lax
from jax.experimental import pallas as pl
from jax.experimental.pallas import tpu as pltpu
from jax.sharding import PartitionSpec as P

MESH = pl.DeviceIdType.MESH
F32 = jnp.float32
BF16 = jnp.bfloat16
FIXED = 65535.0


def threshold_constants(count):
    diameter = 4e-05 * np.power(1.35, np.arange(count))
    return np.sqrt(0.0123 * (2160.0 * 9.81 * diameter + 0.0003 / (1.227 * diameter)))


def rows_of(values, shape):
    row = lax.broadcasted_iota(jnp.int32, shape, 0)
    total = jnp.zeros(shape, F32)
    for r, value in enumerate(values):
        total = jnp.where(row == r, value, total)
    return total


def kernel(
    n, nt, nblocks, ncells, columns, nbins, nsalt, ntex, levels,
    wind_hbm, moist_hbm, tex_hbm, index_hbm, map_hbm, frac_hbm, blast_hbm, dest_hbm,
    w_hbm, atm_hbm, dust_hbm, mix_hbm, settle_hbm,
    land_out, dust_out,
    wind, moist, tex, index, soil, frac, blast, dest_v, dest_s, w, atm, dust, mix, settle,
    packed, erod, root, coef, emitted, part, sums, send, came, mine, gath, numer, base, gain,
    in_sem, w_sem, surf_send, surf_recv, flux_send, flux_recv,
):
    half = columns // 2
    me = lax.axis_index("sec") * nt + lax.axis_index("tile")

    def local(src, dst, k):
        copy = pltpu.make_async_copy(src, dst, in_sem.at[k])
        copy.start()
        return copy

    copies = [
        local(src, dst, k)
        for k, (src, dst) in enumerate(
            [
                (mix_hbm, mix), (atm_hbm, atm), (map_hbm, soil), (index_hbm, index),
                (dust_hbm.at[:, 0:half], dust.at[0]), (dust_hbm.at[:, half:columns], dust.at[1]),
                (wind_hbm, wind), (moist_hbm, moist), (tex_hbm, tex), (frac_hbm, frac),
                (blast_hbm, blast), (dest_hbm, dest_v), (dest_hbm, dest_s), (settle_hbm, settle),
            ]
        )
    ]
    groups = nblocks // 8

    def peer(i):
        p = lax.rem(me + i, n)
        return p, (p // nt, lax.rem(p, nt))

    barrier = pltpu.get_barrier_semaphore()

    def greet(i, carry):
        pl.semaphore_signal(barrier, inc=1, device_id=peer(i)[1], device_id_type=MESH)
        return carry

    lax.fori_loop(1, n, greet, 0)

    def chunk(i):
        at = pl.ds(i * 8, 8)
        return pltpu.make_async_copy(w_hbm.at[at], w.at[at], w_sem.at[i])

    def fetch(i, carry):
        chunk(i).start()
        return carry

    lax.fori_loop(0, groups, fetch, 0)
    for copy in copies:
        copy.wait()

    sink = rows_of([settle[0, f] for f in range(nbins)], (nbins, columns))
    above = None
    held = [None] * 3
    ratios = [None] * levels
    values = [None] * levels
    for level in range(levels - 1, -1, -1):
        pivot = jnp.ones((1, columns), F32)
        dust_pivot = jnp.ones((nbins, columns), F32)
        at = pl.ds(level, nbins, stride=levels)
        dust_right = jnp.concatenate([dust[0, at, :], dust[1, at, :]], axis=1)
        low = up = dust_low = None
        if level > 0:
            low = mix[level - 1:level, :]
            dust_low = jnp.broadcast_to(low, (nbins, columns))
            pivot = pivot + low
            dust_pivot = dust_pivot + dust_low
        if level < levels - 1:
            up = mix[level:level + 1, :]
            pivot = pivot + up * (1.0 - above)
            dust_up = jnp.broadcast_to(up, (nbins, columns)) + sink
            dust_pivot = dust_pivot + dust_up * (1.0 - ratios[level + 1])
            dust_right = dust_right + dust_up * values[level + 1]
        else:
            dust_pivot = dust_pivot + sink
        inverse = 1.0 / pivot
        dust_inverse = 1.0 / dust_pivot
        for f in range(3):
            right = atm[f, level:level + 1, :]
            if up is not None:
                right = right + up * held[f]
            held[f] = right * inverse
        values[level] = dust_right * dust_inverse
        if low is not None:
            above = low * inverse
            ratios[level] = dust_low * dust_inverse
    speed = jnp.sqrt(held[0] * held[0] + held[1] * held[1] + 0.25)
    mine[0:1, :] = speed.astype(BF16).astype(F32)
    mine[1:2, :] = held[2].astype(BF16).astype(F32)
    scale = float(columns) / float(ncells * nblocks)
    now, step = values[0], dust_inverse * scale
    base[0], gain[0] = now, step
    for level in range(1, levels):
        now = values[level] + ratios[level] * now
        step = ratios[level] * step
        base[level], gain[level] = now, step

    words = soil.shape[0] // 2
    fixed = jnp.floor(soil[...] * FIXED + 0.5).astype(jnp.int32)
    packed[...] = fixed[:words] + (fixed[words:] << 16)
    bits = words.bit_length() - 1

    coef[...] = jnp.zeros_like(coef)
    for t in range(ntex):
        coef[:, 16 * t:16 * t + nsalt] = 40.0 * blast[t] * frac[t:t + 1, :]
    root[...] = jnp.sqrt(1.0 + 12.1 * moist[...])

    pl.semaphore_wait(barrier, n - 1)

    def send_surface(i, carry):
        pltpu.make_async_remote_copy(
            src_ref=mine, dst_ref=gath.at[me], send_sem=surf_send, recv_sem=surf_recv,
            device_id=peer(i)[1], device_id_type=MESH,
        ).start()
        return carry

    lax.fori_loop(1, n, send_surface, 0)
    gath[me] = mine[...]

    full = coef[:, 0:16 * ntex]
    coarse = full.astype(BF16)
    fine = (full - coarse.astype(F32)).astype(BF16)
    table = jnp.concatenate([coarse, fine], axis=0)
    thresh0 = rows_of([float(v) for v in threshold_constants(nsalt)], (16, ncells))
    nothing = jnp.zeros((nbins, ncells), F32)

    def erode(i):
        at = pl.ds(pl.multiple_of(i * 8, 8), 8)
        cell = index[at, :]
        lane = cell & 127
        row = cell >> 7
        picks = [((row >> b) & 1) == 1 for b in range(bits)]

        def tree(bit, first):
            if bit < 0:
                words_row = jnp.broadcast_to(packed[first:first + 1, :], (8, 128))
                return jnp.take_along_axis(words_row, lane, axis=1, mode="promise_in_bounds")
            return jnp.where(picks[bit], tree(bit - 1, first + (1 << bit)), tree(bit - 1, first))

        word = tree(bits - 1, 0)
        value = jnp.where(row >= words, lax.shift_right_logical(word, 16), word) & 65535
        erod[at, :] = value.astype(F32) * (1.0 / FIXED)

    def emit(i):
        blocks = []
        for j in range(8):
            at = pl.ds(i * 8 + j, 1)
            speed_row = jnp.broadcast_to(wind[at, :], (16, ncells))
            thresh = thresh0 * jnp.broadcast_to(root[at, :], (16, ncells))
            total = speed_row + thresh
            salt = jnp.broadcast_to(erod[at, :], (16, ncells)) * total * (
                total * jnp.maximum(speed_row - thresh, 0.0)
            )
            kind = jnp.broadcast_to(tex[at, :], (16, ncells))
            blocks.append(
                jnp.concatenate(
                    [jnp.where(kind == t, salt, 0.0).astype(BF16) for t in range(ntex)], axis=0
                )
            )
        both = jnp.dot(table, jnp.concatenate(blocks, axis=1), preferred_element_type=F32)
        emission = both[0:nbins] + both[nbins:2 * nbins]
        for j in range(0, 8, 2):
            first = emission[:, j * ncells:(j + 1) * ncells]
            second = emission[:, (j + 1) * ncells:(j + 2) * ncells]
            left = jnp.concatenate(
                [
                    jnp.concatenate([first, nothing], axis=1),
                    jnp.concatenate([nothing, second], axis=1),
                ],
                axis=0,
            )
            at = pl.ds(pl.multiple_of((i * 4 + j // 2) * 16, 16), 16)
            emitted[at, :] = left.astype(BF16)

    def regrid(i):
        for j in range(0, 8, 2):
            at = pl.ds(pl.multiple_of((i * 4 + j // 2) * 16, 16), 16)
            weights = w[pl.ds(i * 8 + j, 2)].reshape(2 * ncells, columns)
            flux = jnp.dot(emitted[at, :], weights, preferred_element_type=F32)
            for s in range(2):
                at = pl.ds(i * 8 + j + s, nbins, stride=nblocks)
                part[0, at, :] = flux[s * nbins:(s + 1) * nbins, 0:half]
                part[1, at, :] = flux[s * nbins:(s + 1) * nbins, half:columns]

    erode(0)
    emit(0)
    erode(1)

    def steps(i, carry):
        chunk(i - 2).wait()
        regrid(i - 2)
        emit(i - 1)
        erode(i)
        return carry

    lax.fori_loop(2, groups, steps, 0)
    chunk(groups - 2).wait()
    chunk(groups - 1).wait()
    regrid(groups - 2)
    emit(groups - 1)
    regrid(groups - 1)

    tiles = lax.broadcasted_iota(jnp.int32, (n, nblocks), 0)
    placing = jnp.where(jnp.broadcast_to(dest_v[...], (n, nblocks)) == tiles, 1.0, 0.0).astype(BF16)
    placing = jnp.concatenate([placing, placing], axis=1)
    for k in range(nbins):
        at = slice(k * nblocks, (k + 1) * nblocks)
        block = jnp.concatenate([part[0, at, :], part[1, at, :]], axis=1)
        high = block.astype(BF16)
        low = (block - high.astype(F32)).astype(BF16)
        total = jnp.dot(placing, jnp.concatenate([high, low], axis=0), preferred_element_type=F32)
        sums[pl.ds(k, n, stride=2 * nbins), :] = total[:, 0:half]
        sums[pl.ds(nbins + k, n, stride=2 * nbins), :] = total[:, half:columns]
    send[...] = sums[...].reshape(n, 2 * nbins, half).astype(BF16)

    def send_flux(i, carry):
        p, target = peer(i)
        pltpu.make_async_remote_copy(
            src_ref=send.at[p], dst_ref=came.at[me], send_sem=flux_send, recv_sem=flux_recv,
            device_id=target, device_id_type=MESH,
        ).start()
        return carry

    lax.fori_loop(1, n, send_flux, 0)
    came[me] = send[me]

    arrived = gath.at[pl.ds(0, n - 1)]
    pltpu.make_async_copy(arrived, arrived, surf_recv).wait()
    rest = jnp.where(lax.broadcasted_iota(jnp.int32, (6, columns), 0) == 0, 1.0, 0.0)

    def back(i, carry):
        for j in range(0, 16, 2):
            g = i * 16 + j
            left = jnp.concatenate(
                [gath[dest_s[0, g]], rest, gath[dest_s[0, g + 1]], rest], axis=0
            ).astype(BF16)
            weights = w[pl.ds(g, 2)].reshape(2 * ncells, columns)
            found = lax.dot_general(
                left, weights, (((1,), (1,)), ((), ())), preferred_element_type=F32
            )
            numer[pl.ds(pl.multiple_of(g * 8, 8), 8), :] = found[0:8, 0:ncells]
            numer[pl.ds(pl.multiple_of(g * 8 + 8, 8), 8), :] = found[8:16, ncells:2 * ncells]
        return carry

    lax.fori_loop(0, groups // 2, back, 0)
    weight = 1.0 / numer[pl.ds(2, nblocks, stride=8), :]
    land_out[0] = numer[pl.ds(0, nblocks, stride=8), :] * weight
    land_out[1] = 0.5 * moist[...] + 0.5 * (numer[pl.ds(1, nblocks, stride=8), :] * weight)

    landed = came.at[pl.ds(0, n - 1)]
    pltpu.make_async_copy(landed, landed, flux_recv).wait()
    flux = jnp.sum(came[...].astype(F32), axis=0)
    flux = jnp.concatenate([flux[0:nbins], flux[nbins:2 * nbins]], axis=1)
    for level in range(levels):
        dust_out[:, level, :] = base[level] + gain[level] * flux

    sent = gath.at[pl.ds(0, n - 1)]
    pltpu.make_async_copy(sent, sent, surf_send).wait()
    gone = came.at[pl.ds(0, n - 1)]
    pltpu.make_async_copy(gone, gone, flux_send).wait()


def on_device(
    nt, land_wind, land_moist, texture, land_index, erod_map, mass_frac, blast_table, dest_tile,
    regrid_w, atm_state, dust_mix, mixing, settle,
):
    nblocks, ncells = land_wind.shape
    columns = regrid_w.shape[2]
    ntex, nbins, nsalt = blast_table.shape
    levels = atm_state.shape[1]
    half = columns // 2
    n = lax.axis_size(("sec", "tile"))
    groups = nblocks // 8
    soil = erod_map.reshape(-1, 128)
    land = pltpu.VMEM((nblocks, ncells), F32)
    whole = pltpu.VMEM((nblocks, ncells), jnp.int32)
    return pl.pallas_call(
        functools.partial(kernel, n, nt, nblocks, ncells, columns, nbins, nsalt, ntex, levels),
        out_shape=(
            jax.ShapeDtypeStruct((2, nblocks, ncells), F32),
            jax.ShapeDtypeStruct((nbins, levels, columns), F32),
        ),
        in_specs=[pl.BlockSpec(memory_space=pltpu.HBM)] * 13,
        out_specs=(pl.BlockSpec(memory_space=pltpu.VMEM), pl.BlockSpec(memory_space=pltpu.VMEM)),
        scratch_shapes=[
            land,
            land,
            whole,
            whole,
            pltpu.VMEM(soil.shape, F32),
            pltpu.VMEM(mass_frac.shape, F32),
            pltpu.VMEM(blast_table.shape, F32),
            pltpu.VMEM((1, nblocks), jnp.int32),
            pltpu.SMEM((1, nblocks), jnp.int32),
            pltpu.VMEM(regrid_w.shape, BF16),
            pltpu.VMEM(atm_state.shape, F32),
            pltpu.VMEM((2, nbins * levels, half), F32),
            pltpu.VMEM(mixing.shape, F32),
            pltpu.SMEM((1, nbins), F32),
            pltpu.VMEM((soil.shape[0] // 2, 128), jnp.int32),
            land,
            land,
            pltpu.VMEM((nbins, 128), F32),
            pltpu.VMEM((nblocks * nbins, columns), BF16),
            pltpu.VMEM((2, nbins * nblocks, half), F32),
            pltpu.VMEM((n * 2 * nbins, half), F32),
            pltpu.VMEM((n, 2 * nbins, half), BF16),
            pltpu.VMEM((n, 2 * nbins, half), BF16),
            pltpu.VMEM((2, columns), F32),
            pltpu.VMEM((n, 2, columns), F32),
            pltpu.VMEM((nblocks * 8, ncells), F32),
            pltpu.VMEM((levels, nbins, columns), F32),
            pltpu.VMEM((levels, nbins, columns), F32),
            pltpu.SemaphoreType.DMA((14,)),
            pltpu.SemaphoreType.DMA((groups,)),
            pltpu.SemaphoreType.DMA,
            pltpu.SemaphoreType.DMA,
            pltpu.SemaphoreType.DMA,
            pltpu.SemaphoreType.DMA,
        ],
        compiler_params=pltpu.CompilerParams(
            collective_id=0, has_side_effects=True, vmem_limit_bytes=60 * 1024 * 1024
        ),
    )(
        land_wind, land_moist, texture, land_index, soil, mass_frac, blast_table,
        dest_tile.reshape(1, nblocks), regrid_w, atm_state,
        dust_mix.reshape(nbins * levels, columns), mixing, settle.reshape(1, nbins),
    )


def solution(mesh):
    both = ("sec", "tile")
    in_specs = (
        P(both, None),
        P(both, None),
        P(both, None),
        P(both, None),
        P(both),
        P(),
        P(),
        P(both, None),
        P(both, None, None),
        P(None, None, both),
        P(None, None, both),
        P(None, both),
        P(),
    )
    out_specs = (P(None, both, None), P(None, None, both))
    return jax.shard_map(
        functools.partial(on_device, mesh.shape["tile"]),
        mesh=mesh, in_specs=in_specs, out_specs=out_specs, check_vma=False,
    )
```

```python
import functools

import jax
import jax.numpy as jnp
import numpy as np
from jax import lax
from jax.experimental import pallas as pl
from jax.experimental.pallas import tpu as pltpu
from jax.sharding import PartitionSpec as P

MESH = pl.DeviceIdType.MESH
F32 = jnp.float32
BF16 = jnp.bfloat16
FIXED = 65535.0


def threshold_constants(count):
    diameter = 4e-05 * np.power(1.35, np.arange(count))
    return np.sqrt(0.0123 * (2160.0 * 9.81 * diameter + 0.0003 / (1.227 * diameter)))


def rows_of(values, shape):
    row = lax.broadcasted_iota(jnp.int32, shape, 0)
    total = jnp.zeros(shape, F32)
    for r, value in enumerate(values):
        total = jnp.where(row == r, value, total)
    return total


def kernel(
    n, nt, nblocks, ncells, columns, nbins, nsalt, ntex, levels,
    wind_hbm, moist_hbm, tex_hbm, index_hbm, map_hbm, frac_hbm, blast_hbm, dest_hbm,
    w_hbm, atm_hbm, dust_hbm, mix_hbm, settle_hbm,
    results,
    wind, moist, tex, index, soil, frac, blast, dest_v, dest_s, w, atm, dust, mix, settle,
    packed, erod, root, coef, emitted, part, sums, send, came, mine, gath, numer, base, gain,
    in_sem, w_sem, surf_send, surf_recv, flux_send, flux_recv,
):
    half = columns // 2
    me = lax.axis_index("sec") * nt + lax.axis_index("tile")

    def local(src, dst, k):
        copy = pltpu.make_async_copy(src, dst, in_sem.at[k])
        copy.start()
        return copy

    copies = [
        local(src, dst, k)
        for k, (src, dst) in enumerate(
            [
                (mix_hbm, mix), (atm_hbm, atm), (map_hbm, soil), (index_hbm, index),
                (dust_hbm.at[:, 0:half], dust.at[0]), (dust_hbm.at[:, half:columns], dust.at[1]),
                (wind_hbm, wind), (moist_hbm, moist), (tex_hbm, tex), (frac_hbm, frac),
                (blast_hbm, blast), (dest_hbm, dest_v), (dest_hbm, dest_s), (settle_hbm, settle),
            ]
        )
    ]
    groups = nblocks // 8

    def peer(i):
        p = lax.rem(me + i, n)
        return p, (p // nt, lax.rem(p, nt))

    barrier = pltpu.get_barrier_semaphore()

    def greet(i, carry):
        pl.semaphore_signal(barrier, inc=1, device_id=peer(i)[1], device_id_type=MESH)
        return carry

    lax.fori_loop(1, n, greet, 0)

    def chunk(i):
        at = pl.ds(i * 8, 8)
        return pltpu.make_async_copy(w_hbm.at[at], w.at[at], w_sem.at[i])

    def fetch(i, carry):
        chunk(i).start()
        return carry

    lax.fori_loop(0, groups, fetch, 0)
    for copy in copies:
        copy.wait()

    sink = rows_of([settle[0, f] for f in range(nbins)], (nbins, columns))
    above = None
    held = [None] * 3
    ratios = [None] * levels
    values = [None] * levels
    for level in range(levels - 1, -1, -1):
        pivot = jnp.ones((1, columns), F32)
        dust_pivot = jnp.ones((nbins, columns), F32)
        at = pl.ds(level, nbins, stride=levels)
        dust_right = jnp.concatenate([dust[0, at, :], dust[1, at, :]], axis=1)
        low = up = dust_low = None
        if level > 0:
            low = mix[level - 1:level, :]
            dust_low = jnp.broadcast_to(low, (nbins, columns))
            pivot = pivot + low
            dust_pivot = dust_pivot + dust_low
        if level < levels - 1:
            up = mix[level:level + 1, :]
            pivot = pivot + up * (1.0 - above)
            dust_up = jnp.broadcast_to(up, (nbins, columns)) + sink
            dust_pivot = dust_pivot + dust_up * (1.0 - ratios[level + 1])
            dust_right = dust_right + dust_up * values[level + 1]
        else:
            dust_pivot = dust_pivot + sink
        inverse = 1.0 / pivot
        dust_inverse = 1.0 / dust_pivot
        for f in range(3):
            right = atm[f, level:level + 1, :]
            if up is not None:
                right = right + up * held[f]
            held[f] = right * inverse
        values[level] = dust_right * dust_inverse
        if low is not None:
            above = low * inverse
            ratios[level] = dust_low * dust_inverse
    speed = jnp.sqrt(held[0] * held[0] + held[1] * held[1] + 0.25)
    mine[0:1, :] = speed.astype(BF16).astype(F32)
    mine[1:2, :] = held[2].astype(BF16).astype(F32)
    scale = float(columns) / float(ncells * nblocks)
    now, step = values[0], dust_inverse * scale
    base[0], gain[0] = now, step
    for level in range(1, levels):
        now = values[level] + ratios[level] * now
        step = ratios[level] * step
        base[level], gain[level] = now, step

    words = soil.shape[0] // 2
    fixed = jnp.floor(soil[...] * FIXED + 0.5).astype(jnp.int32)
    packed[...] = fixed[:words] + (fixed[words:] << 16)
    bits = words.bit_length() - 1

    coef[...] = jnp.zeros_like(coef)
    for t in range(ntex):
        coef[:, 16 * t:16 * t + nsalt] = 40.0 * blast[t] * frac[t:t + 1, :]
    root[...] = jnp.sqrt(1.0 + 12.1 * moist[...])

    pl.semaphore_wait(barrier, n - 1)

    def send_surface(i, carry):
        pltpu.make_async_remote_copy(
            src_ref=mine, dst_ref=gath.at[me], send_sem=surf_send, recv_sem=surf_recv,
            device_id=peer(i)[1], device_id_type=MESH,
        ).start()
        return carry

    lax.fori_loop(1, n, send_surface, 0)
    gath[me] = mine[...]

    full = coef[:, 0:16 * ntex]
    coarse = full.astype(BF16)
    fine = (full - coarse.astype(F32)).astype(BF16)
    table = jnp.concatenate([coarse, fine], axis=0)
    thresh0 = rows_of([float(v) for v in threshold_constants(nsalt)], (16, ncells))
    nothing = jnp.zeros((nbins, ncells), F32)

    def erode(i):
        at = pl.ds(pl.multiple_of(i * 8, 8), 8)
        cell = index[at, :]
        lane = cell & 127
        row = cell >> 7
        picks = [((row >> b) & 1) == 1 for b in range(bits)]

        def tree(bit, first):
            if bit < 0:
                words_row = jnp.broadcast_to(packed[first:first + 1, :], (8, 128))
                return jnp.take_along_axis(words_row, lane, axis=1, mode="promise_in_bounds")
            return jnp.where(picks[bit], tree(bit - 1, first + (1 << bit)), tree(bit - 1, first))

        word = tree(bits - 1, 0)
        value = jnp.where(row >= words, lax.shift_right_logical(word, 16), word) & 65535
        erod[at, :] = value.astype(F32) * (1.0 / FIXED)

    def emit(i):
        blocks = []
        for j in range(8):
            at = pl.ds(i * 8 + j, 1)
            speed_row = jnp.broadcast_to(wind[at, :], (16, ncells))
            thresh = thresh0 * jnp.broadcast_to(root[at, :], (16, ncells))
            total = speed_row + thresh
            salt = jnp.broadcast_to(erod[at, :], (16, ncells)) * total * (
                total * jnp.maximum(speed_row - thresh, 0.0)
            )
            kind = jnp.broadcast_to(tex[at, :], (16, ncells))
            blocks.append(
                jnp.concatenate(
                    [jnp.where(kind == t, salt, 0.0).astype(BF16) for t in range(ntex)], axis=0
                )
            )
        both = jnp.dot(table, jnp.concatenate(blocks, axis=1), preferred_element_type=F32)
        emission = both[0:nbins] + both[nbins:2 * nbins]
        for j in range(0, 8, 2):
            first = emission[:, j * ncells:(j + 1) * ncells]
            second = emission[:, (j + 1) * ncells:(j + 2) * ncells]
            left = jnp.concatenate(
                [
                    jnp.concatenate([first, nothing], axis=1),
                    jnp.concatenate([nothing, second], axis=1),
                ],
                axis=0,
            )
            at = pl.ds(pl.multiple_of((i * 4 + j // 2) * 16, 16), 16)
            emitted[at, :] = left.astype(BF16)

    def regrid(i):
        for j in range(0, 8, 2):
            at = pl.ds(pl.multiple_of((i * 4 + j // 2) * 16, 16), 16)
            weights = w[pl.ds(i * 8 + j, 2)].reshape(2 * ncells, columns)
            flux = jnp.dot(emitted[at, :], weights, preferred_element_type=F32)
            for s in range(2):
                at = pl.ds(i * 8 + j + s, nbins, stride=nblocks)
                part[0, at, :] = flux[s * nbins:(s + 1) * nbins, 0:half]
                part[1, at, :] = flux[s * nbins:(s + 1) * nbins, half:columns]

    erode(0)
    emit(0)
    erode(1)

    def steps(i, carry):
        chunk(i - 2).wait()
        regrid(i - 2)
        emit(i - 1)
        erode(i)
        return carry

    lax.fori_loop(2, groups, steps, 0)
    chunk(groups - 2).wait()
    chunk(groups - 1).wait()
    regrid(groups - 2)
    emit(groups - 1)
    regrid(groups - 1)

    tiles = lax.broadcasted_iota(jnp.int32, (n, nblocks), 0)
    placing = jnp.where(jnp.broadcast_to(dest_v[...], (n, nblocks)) == tiles, 1.0, 0.0).astype(BF16)
    placing = jnp.concatenate([placing, placing], axis=1)
    for k in range(nbins):
        at = slice(k * nblocks, (k + 1) * nblocks)
        block = jnp.concatenate([part[0, at, :], part[1, at, :]], axis=1)
        high = block.astype(BF16)
        low = (block - high.astype(F32)).astype(BF16)
        total = jnp.dot(placing, jnp.concatenate([high, low], axis=0), preferred_element_type=F32)
        sums[pl.ds(k, n, stride=2 * nbins), :] = total[:, 0:half]
        sums[pl.ds(nbins + k, n, stride=2 * nbins), :] = total[:, half:columns]
    send[...] = sums[...].reshape(n, 2 * nbins, half).astype(BF16)

    def send_flux(i, carry):
        p, target = peer(i)
        pltpu.make_async_remote_copy(
            src_ref=send.at[p], dst_ref=came.at[me], send_sem=flux_send, recv_sem=flux_recv,
            device_id=target, device_id_type=MESH,
        ).start()
        return carry

    lax.fori_loop(1, n, send_flux, 0)
    came[me] = send[me]

    arrived = gath.at[pl.ds(0, n - 1)]
    pltpu.make_async_copy(arrived, arrived, surf_recv).wait()
    rest = jnp.where(lax.broadcasted_iota(jnp.int32, (6, columns), 0) == 0, 1.0, 0.0)

    def back(i, carry):
        for j in range(0, 16, 2):
            g = i * 16 + j
            left = jnp.concatenate(
                [gath[dest_s[0, g]], rest, gath[dest_s[0, g + 1]], rest], axis=0
            ).astype(BF16)
            weights = w[pl.ds(g, 2)].reshape(2 * ncells, columns)
            found = lax.dot_general(
                left, weights, (((1,), (1,)), ((), ())), preferred_element_type=F32
            )
            numer[pl.ds(pl.multiple_of(g * 8, 8), 8), :] = found[0:8, 0:ncells]
            numer[pl.ds(pl.multiple_of(g * 8 + 8, 8), 8), :] = found[8:16, ncells:2 * ncells]
        return carry

    lax.fori_loop(0, groups // 2, back, 0)
    weight = 1.0 / numer[pl.ds(2, nblocks, stride=8), :]
    results[0:nblocks, :] = numer[pl.ds(0, nblocks, stride=8), :] * weight
    results[nblocks:2 * nblocks, :] = 0.5 * moist[...] + 0.5 * (numer[pl.ds(1, nblocks, stride=8), :] * weight)

    landed = came.at[pl.ds(0, n - 1)]
    pltpu.make_async_copy(landed, landed, flux_recv).wait()
    flux = jnp.sum(came[...].astype(F32), axis=0)
    flux = jnp.concatenate([flux[0:nbins], flux[nbins:2 * nbins]], axis=1)
    for level in range(levels):
        total = base[level] + gain[level] * flux
        for h in range(2):
            first = 2 * nblocks + h * nbins * levels + level
            results[pl.ds(first, nbins, stride=levels), :] = total[:, h * half:(h + 1) * half]

    sent = gath.at[pl.ds(0, n - 1)]
    pltpu.make_async_copy(sent, sent, surf_send).wait()
    gone = came.at[pl.ds(0, n - 1)]
    pltpu.make_async_copy(gone, gone, flux_send).wait()


def unpack(nblocks, half, results, land_out, dust_out, sem):
    rows = dust_out.shape[0]
    copies = [
        pltpu.make_async_copy(results.at[pl.ds(0, 2 * nblocks)], land_out, sem.at[0]),
        pltpu.make_async_copy(
            results.at[pl.ds(2 * nblocks, rows)], dust_out.at[:, 0:half], sem.at[1]
        ),
        pltpu.make_async_copy(
            results.at[pl.ds(2 * nblocks + rows, rows)], dust_out.at[:, half:2 * half], sem.at[2]
        ),
    ]
    for copy in copies:
        copy.start()
    for copy in copies:
        copy.wait()


def on_device(
    nt, land_wind, land_moist, texture, land_index, erod_map, mass_frac, blast_table, dest_tile,
    regrid_w, atm_state, dust_mix, mixing, settle,
):
    nblocks, ncells = land_wind.shape
    columns = regrid_w.shape[2]
    ntex, nbins, nsalt = blast_table.shape
    levels = atm_state.shape[1]
    half = columns // 2
    n = lax.axis_size(("sec", "tile"))
    groups = nblocks // 8
    soil = erod_map.reshape(-1, 128)
    operands = (
        land_wind, land_moist, texture, land_index, soil, mass_frac, blast_table,
        dest_tile.reshape(1, nblocks), regrid_w, atm_state,
        dust_mix.reshape(nbins * levels, columns), mixing, settle.reshape(1, nbins),
    )
    land = pltpu.VMEM((nblocks, ncells), F32)
    whole = pltpu.VMEM((nblocks, ncells), jnp.int32)
    results = pl.pallas_call(
        functools.partial(kernel, n, nt, nblocks, ncells, columns, nbins, nsalt, ntex, levels),
        out_shape=jax.ShapeDtypeStruct((2 * nblocks + 2 * nbins * levels, 128), F32),
        in_specs=[pl.BlockSpec(memory_space=pltpu.HBM)] * 13,
        out_specs=pl.BlockSpec(memory_space=pltpu.VMEM),
        scratch_shapes=[
            land,
            land,
            whole,
            whole,
            pltpu.VMEM(soil.shape, F32),
            pltpu.VMEM(mass_frac.shape, F32),
            pltpu.VMEM(blast_table.shape, F32),
            pltpu.VMEM((1, nblocks), jnp.int32),
            pltpu.SMEM((1, nblocks), jnp.int32),
            pltpu.VMEM(regrid_w.shape, BF16),
            pltpu.VMEM(atm_state.shape, F32),
            pltpu.VMEM((2, nbins * levels, half), F32),
            pltpu.VMEM(mixing.shape, F32),
            pltpu.SMEM((1, nbins), F32),
            pltpu.VMEM((soil.shape[0] // 2, 128), jnp.int32),
            land,
            land,
            pltpu.VMEM((nbins, 128), F32),
            pltpu.VMEM((nblocks * nbins, columns), BF16),
            pltpu.VMEM((2, nbins * nblocks, half), F32),
            pltpu.VMEM((n * 2 * nbins, half), F32),
            pltpu.VMEM((n, 2 * nbins, half), BF16),
            pltpu.VMEM((n, 2 * nbins, half), BF16),
            pltpu.VMEM((2, columns), F32),
            pltpu.VMEM((n, 2, columns), F32),
            pltpu.VMEM((nblocks * 8, ncells), F32),
            pltpu.VMEM((levels, nbins, columns), F32),
            pltpu.VMEM((levels, nbins, columns), F32),
            pltpu.SemaphoreType.DMA((14,)),
            pltpu.SemaphoreType.DMA((groups,)),
            pltpu.SemaphoreType.DMA,
            pltpu.SemaphoreType.DMA,
            pltpu.SemaphoreType.DMA,
            pltpu.SemaphoreType.DMA,
        ],
        compiler_params=pltpu.CompilerParams(
            collective_id=0, has_side_effects=True, vmem_limit_bytes=40 * 1024 * 1024
        ),
    )(*(pltpu.with_memory_space_constraint(x, pltpu.HBM) for x in operands))
    land_out, dust_out = pl.pallas_call(
        functools.partial(unpack, nblocks, half),
        out_shape=(
            jax.ShapeDtypeStruct((2 * nblocks, ncells), F32),
            jax.ShapeDtypeStruct((nbins * levels, columns), F32),
        ),
        in_specs=[pl.BlockSpec(memory_space=pl.ANY)],
        out_specs=(pl.BlockSpec(memory_space=pltpu.HBM), pl.BlockSpec(memory_space=pltpu.HBM)),
        scratch_shapes=[pltpu.SemaphoreType.DMA((3,))],
    )(results)
    return land_out.reshape(2, nblocks, ncells), dust_out.reshape(nbins, levels, columns)


def solution(mesh):
    both = ("sec", "tile")
    in_specs = (
        P(both, None),
        P(both, None),
        P(both, None),
        P(both, None),
        P(both),
        P(),
        P(),
        P(both, None),
        P(both, None, None),
        P(None, None, both),
        P(None, None, both),
        P(None, both),
        P(),
    )
    out_specs = (P(None, both, None), P(None, None, both))
    return jax.shard_map(
        functools.partial(on_device, mesh.shape["tile"]),
        mesh=mesh, in_specs=in_specs, out_specs=out_specs, check_vma=False,
    )
```

```python
import functools

import jax
import jax.numpy as jnp
import numpy as np
from jax import lax
from jax.experimental import pallas as pl
from jax.experimental.pallas import tpu as pltpu
from jax.sharding import PartitionSpec as P

FLAT = pl.DeviceIdType.LOGICAL
STEP = 4
F32 = jnp.float32
BF16 = jnp.bfloat16
FIXED = 65535.0


def threshold_constants(count):
    diameter = 4e-05 * np.power(1.35, np.arange(count))
    return np.sqrt(0.0123 * (2160.0 * 9.81 * diameter + 0.0003 / (1.227 * diameter)))


def rows_of(values, shape):
    row = lax.broadcasted_iota(jnp.int32, shape, 0)
    total = jnp.zeros(shape, F32)
    for r, value in enumerate(values):
        total = jnp.where(row == r, value, total)
    return total


def kernel(
    n, nt, nblocks, ncells, columns, nbins, nsalt, ntex, levels,
    wind_hbm, moist_hbm, tex_hbm, index_hbm, map_hbm, frac_hbm, blast_hbm, dest_hbm,
    w_hbm, atm_hbm, dust_hbm, mix_hbm, settle_hbm,
    results,
    wind, moist, tex, index, soil, frac, blast, dest_v, dest_s, w, atm, dust, mix, settle,
    packed, erod, root, coef, emitted, part, sums, send, came, mine, gath, numer, base, gain,
    in_sem, w_sem, surf_send, surf_recv, flux_send, flux_recv,
):
    half = columns // 2
    me = lax.axis_index("sec") * nt + lax.axis_index("tile")

    def local(src, dst, k):
        copy = pltpu.make_async_copy(src, dst, in_sem.at[k])
        copy.start()
        return copy

    copies = [
        local(src, dst, k)
        for k, (src, dst) in enumerate(
            [
                (mix_hbm, mix), (atm_hbm, atm), (map_hbm, soil), (index_hbm, index),
                (dust_hbm.at[:, 0:half], dust.at[0]), (dust_hbm.at[:, half:columns], dust.at[1]),
                (wind_hbm, wind), (moist_hbm, moist), (tex_hbm, tex), (frac_hbm, frac),
                (blast_hbm, blast), (dest_hbm, dest_v), (dest_hbm, dest_s), (settle_hbm, settle),
            ]
        )
    ]
    groups = nblocks // 8

    def each_peer(act):
        def several(i, carry):
            for j in range(STEP):
                one(i * STEP + j + 1)
            return carry

        def one(i):
            p = me + i
            act(jnp.where(p >= n, p - n, p))

        lax.fori_loop(0, (n - 1) // STEP, several, 0)
        for i in range((n - 1) // STEP * STEP + 1, n):
            one(i)

    barrier = pltpu.get_barrier_semaphore()

    def greet(p):
        pl.semaphore_signal(barrier, inc=1, device_id=p, device_id_type=FLAT)

    each_peer(greet)

    def chunk(i):
        at = pl.ds(i * 8, 8)
        return pltpu.make_async_copy(w_hbm.at[at], w.at[at], w_sem.at[i])

    def fetch(i, carry):
        chunk(i).start()
        return carry

    lax.fori_loop(0, groups, fetch, 0)
    for copy in copies:
        copy.wait()

    sink = rows_of([settle[0, f] for f in range(nbins)], (nbins, columns))
    above = None
    held = [None] * 3
    ratios = [None] * levels
    values = [None] * levels
    for level in range(levels - 1, -1, -1):
        pivot = jnp.ones((1, columns), F32)
        dust_pivot = jnp.ones((nbins, columns), F32)
        at = pl.ds(level, nbins, stride=levels)
        dust_right = jnp.concatenate([dust[0, at, :], dust[1, at, :]], axis=1)
        low = up = dust_low = None
        if level > 0:
            low = mix[level - 1:level, :]
            dust_low = jnp.broadcast_to(low, (nbins, columns))
            pivot = pivot + low
            dust_pivot = dust_pivot + dust_low
        if level < levels - 1:
            up = mix[level:level + 1, :]
            pivot = pivot + up * (1.0 - above)
            dust_up = jnp.broadcast_to(up, (nbins, columns)) + sink
            dust_pivot = dust_pivot + dust_up * (1.0 - ratios[level + 1])
            dust_right = dust_right + dust_up * values[level + 1]
        else:
            dust_pivot = dust_pivot + sink
        inverse = 1.0 / pivot
        dust_inverse = 1.0 / dust_pivot
        for f in range(3):
            right = atm[f, level:level + 1, :]
            if up is not None:
                right = right + up * held[f]
            held[f] = right * inverse
        values[level] = dust_right * dust_inverse
        if low is not None:
            above = low * inverse
            ratios[level] = dust_low * dust_inverse
    speed = jnp.sqrt(held[0] * held[0] + held[1] * held[1] + 0.25)
    mine[0:1, :] = speed.astype(BF16).astype(F32)
    mine[1:2, :] = held[2].astype(BF16).astype(F32)
    scale = float(columns) / float(ncells * nblocks)
    now, step = values[0], dust_inverse * scale
    base[0], gain[0] = now, step
    for level in range(1, levels):
        now = values[level] + ratios[level] * now
        step = ratios[level] * step
        base[level], gain[level] = now, step

    words = soil.shape[0] // 2
    fixed = jnp.floor(soil[...] * FIXED + 0.5).astype(jnp.int32)
    packed[...] = fixed[:words] + (fixed[words:] << 16)
    bits = words.bit_length() - 1

    coef[...] = jnp.zeros_like(coef)
    for t in range(ntex):
        coef[:, 16 * t:16 * t + nsalt] = 40.0 * blast[t] * frac[t:t + 1, :]
    root[...] = jnp.sqrt(1.0 + 12.1 * moist[...])

    full = coef[:, 0:16 * ntex]
    coarse = full.astype(BF16)
    fine = (full - coarse.astype(F32)).astype(BF16)
    table = jnp.concatenate([coarse, fine], axis=0)
    thresh0 = rows_of([float(v) for v in threshold_constants(nsalt)], (16, ncells))
    nothing = jnp.zeros((nbins, ncells), F32)

    def erode(i):
        at = pl.ds(pl.multiple_of(i * 8, 8), 8)
        cell = index[at, :]
        lane = cell & 127
        row = cell >> 7
        picks = [((row >> b) & 1) == 1 for b in range(bits)]

        def tree(bit, first):
            if bit < 0:
                words_row = jnp.broadcast_to(packed[first:first + 1, :], (8, 128))
                return jnp.take_along_axis(words_row, lane, axis=1, mode="promise_in_bounds")
            return jnp.where(picks[bit], tree(bit - 1, first + (1 << bit)), tree(bit - 1, first))

        word = tree(bits - 1, 0)
        value = jnp.where(row >= words, lax.shift_right_logical(word, 16), word) & 65535
        erod[at, :] = value.astype(F32) * (1.0 / FIXED)

    def emit(i):
        blocks = []
        for j in range(8):
            at = pl.ds(i * 8 + j, 1)
            speed_row = jnp.broadcast_to(wind[at, :], (16, ncells))
            thresh = thresh0 * jnp.broadcast_to(root[at, :], (16, ncells))
            total = speed_row + thresh
            salt = jnp.broadcast_to(erod[at, :], (16, ncells)) * total * (
                total * jnp.maximum(speed_row - thresh, 0.0)
            )
            kind = jnp.broadcast_to(tex[at, :], (16, ncells))
            blocks.append(
                jnp.concatenate(
                    [jnp.where(kind == t, salt, 0.0).astype(BF16) for t in range(ntex)], axis=0
                )
            )
        both = jnp.dot(table, jnp.concatenate(blocks, axis=1), preferred_element_type=F32)
        emission = both[0:nbins] + both[nbins:2 * nbins]
        for j in range(0, 8, 2):
            first = emission[:, j * ncells:(j + 1) * ncells]
            second = emission[:, (j + 1) * ncells:(j + 2) * ncells]
            left = jnp.concatenate(
                [
                    jnp.concatenate([first, nothing], axis=1),
                    jnp.concatenate([nothing, second], axis=1),
                ],
                axis=0,
            )
            at = pl.ds(pl.multiple_of((i * 4 + j // 2) * 16, 16), 16)
            emitted[at, :] = left.astype(BF16)

    def regrid(i):
        for j in range(0, 8, 2):
            at = pl.ds(pl.multiple_of((i * 4 + j // 2) * 16, 16), 16)
            weights = w[pl.ds(i * 8 + j, 2)].reshape(2 * ncells, columns)
            flux = jnp.dot(emitted[at, :], weights, preferred_element_type=F32)
            for s in range(2):
                at = pl.ds(i * 8 + j + s, nbins, stride=nblocks)
                part[0, at, :] = flux[s * nbins:(s + 1) * nbins, 0:half]
                part[1, at, :] = flux[s * nbins:(s + 1) * nbins, half:columns]

    erode(0)
    emit(0)
    erode(1)

    pl.semaphore_wait(barrier, n - 1)

    def send_surface(p):
        pltpu.make_async_remote_copy(
            src_ref=mine, dst_ref=gath.at[me], send_sem=surf_send, recv_sem=surf_recv,
            device_id=p, device_id_type=FLAT,
        ).start()

    each_peer(send_surface)
    gath[me] = mine[...]

    def steps(i, carry):
        chunk(i - 2).wait()
        regrid(i - 2)
        emit(i - 1)
        erode(i)
        return carry

    lax.fori_loop(2, groups, steps, 0)
    chunk(groups - 2).wait()
    chunk(groups - 1).wait()
    regrid(groups - 2)
    emit(groups - 1)
    regrid(groups - 1)

    tiles = lax.broadcasted_iota(jnp.int32, (n, nblocks), 0)
    placing = jnp.where(jnp.broadcast_to(dest_v[...], (n, nblocks)) == tiles, 1.0, 0.0).astype(BF16)
    placing = jnp.concatenate([placing, placing], axis=1)
    for k in range(nbins):
        at = slice(k * nblocks, (k + 1) * nblocks)
        block = jnp.concatenate([part[0, at, :], part[1, at, :]], axis=1)
        high = block.astype(BF16)
        low = (block - high.astype(F32)).astype(BF16)
        total = jnp.dot(placing, jnp.concatenate([high, low], axis=0), preferred_element_type=F32)
        sums[pl.ds(k, n, stride=2 * nbins), :] = total[:, 0:half]
        sums[pl.ds(nbins + k, n, stride=2 * nbins), :] = total[:, half:columns]
    send[...] = sums[...].reshape(n, 2 * nbins, half).astype(BF16)

    def send_flux(p):
        pltpu.make_async_remote_copy(
            src_ref=send.at[p], dst_ref=came.at[me], send_sem=flux_send, recv_sem=flux_recv,
            device_id=p, device_id_type=FLAT,
        ).start()

    each_peer(send_flux)
    came[me] = send[me]

    arrived = gath.at[pl.ds(0, n - 1)]
    pltpu.make_async_copy(arrived, arrived, surf_recv).wait()
    rest = jnp.where(lax.broadcasted_iota(jnp.int32, (6, columns), 0) == 0, 1.0, 0.0)

    def back(i, carry):
        for j in range(0, 16, 2):
            g = i * 16 + j
            left = jnp.concatenate(
                [gath[dest_s[0, g]], rest, gath[dest_s[0, g + 1]], rest], axis=0
            ).astype(BF16)
            weights = w[pl.ds(g, 2)].reshape(2 * ncells, columns)
            found = lax.dot_general(
                left, weights, (((1,), (1,)), ((), ())), preferred_element_type=F32
            )
            numer[pl.ds(pl.multiple_of(g * 8, 8), 8), :] = found[0:8, 0:ncells]
            numer[pl.ds(pl.multiple_of(g * 8 + 8, 8), 8), :] = found[8:16, ncells:2 * ncells]
        return carry

    lax.fori_loop(0, groups // 2, back, 0)
    weight = 1.0 / numer[pl.ds(2, nblocks, stride=8), :]
    results[0:nblocks, :] = numer[pl.ds(0, nblocks, stride=8), :] * weight
    results[nblocks:2 * nblocks, :] = 0.5 * moist[...] + 0.5 * (numer[pl.ds(1, nblocks, stride=8), :] * weight)

    landed = came.at[pl.ds(0, n - 1)]
    pltpu.make_async_copy(landed, landed, flux_recv).wait()
    flux = jnp.sum(came[...].astype(F32), axis=0)
    flux = jnp.concatenate([flux[0:nbins], flux[nbins:2 * nbins]], axis=1)
    for level in range(levels):
        total = base[level] + gain[level] * flux
        for h in range(2):
            first = 2 * nblocks + h * nbins * levels + level
            results[pl.ds(first, nbins, stride=levels), :] = total[:, h * half:(h + 1) * half]

    sent = gath.at[pl.ds(0, n - 1)]
    pltpu.make_async_copy(sent, sent, surf_send).wait()
    gone = came.at[pl.ds(0, n - 1)]
    pltpu.make_async_copy(gone, gone, flux_send).wait()


def unpack(nblocks, half, results, land_out, dust_out, sem):
    rows = dust_out.shape[0]
    copies = [
        pltpu.make_async_copy(results.at[pl.ds(0, 2 * nblocks)], land_out, sem.at[0]),
        pltpu.make_async_copy(
            results.at[pl.ds(2 * nblocks, rows)], dust_out.at[:, 0:half], sem.at[1]
        ),
        pltpu.make_async_copy(
            results.at[pl.ds(2 * nblocks + rows, rows)], dust_out.at[:, half:2 * half], sem.at[2]
        ),
    ]
    for copy in copies:
        copy.start()
    for copy in copies:
        copy.wait()


def on_device(
    nt, land_wind, land_moist, texture, land_index, erod_map, mass_frac, blast_table, dest_tile,
    regrid_w, atm_state, dust_mix, mixing, settle,
):
    nblocks, ncells = land_wind.shape
    columns = regrid_w.shape[2]
    ntex, nbins, nsalt = blast_table.shape
    levels = atm_state.shape[1]
    half = columns // 2
    n = lax.axis_size(("sec", "tile"))
    groups = nblocks // 8
    soil = erod_map.reshape(-1, 128)
    operands = (
        land_wind, land_moist, texture, land_index, soil, mass_frac, blast_table,
        dest_tile.reshape(1, nblocks), regrid_w, atm_state,
        dust_mix.reshape(nbins * levels, columns), mixing, settle.reshape(1, nbins),
    )
    land = pltpu.VMEM((nblocks, ncells), F32)
    whole = pltpu.VMEM((nblocks, ncells), jnp.int32)
    results = pl.pallas_call(
        functools.partial(kernel, n, nt, nblocks, ncells, columns, nbins, nsalt, ntex, levels),
        out_shape=jax.ShapeDtypeStruct((2 * nblocks + 2 * nbins * levels, 128), F32),
        in_specs=[pl.BlockSpec(memory_space=pltpu.HBM)] * 13,
        out_specs=pl.BlockSpec(memory_space=pltpu.VMEM),
        scratch_shapes=[
            land,
            land,
            whole,
            whole,
            pltpu.VMEM(soil.shape, F32),
            pltpu.VMEM(mass_frac.shape, F32),
            pltpu.VMEM(blast_table.shape, F32),
            pltpu.VMEM((1, nblocks), jnp.int32),
            pltpu.SMEM((1, nblocks), jnp.int32),
            pltpu.VMEM(regrid_w.shape, BF16),
            pltpu.VMEM(atm_state.shape, F32),
            pltpu.VMEM((2, nbins * levels, half), F32),
            pltpu.VMEM(mixing.shape, F32),
            pltpu.SMEM((1, nbins), F32),
            pltpu.VMEM((soil.shape[0] // 2, 128), jnp.int32),
            land,
            land,
            pltpu.VMEM((nbins, 128), F32),
            pltpu.VMEM((nblocks * nbins, columns), BF16),
            pltpu.VMEM((2, nbins * nblocks, half), F32),
            pltpu.VMEM((n * 2 * nbins, half), F32),
            pltpu.VMEM((n, 2 * nbins, half), BF16),
            pltpu.VMEM((n, 2 * nbins, half), BF16),
            pltpu.VMEM((2, columns), F32),
            pltpu.VMEM((n, 2, columns), F32),
            pltpu.VMEM((nblocks * 8, ncells), F32),
            pltpu.VMEM((levels, nbins, columns), F32),
            pltpu.VMEM((levels, nbins, columns), F32),
            pltpu.SemaphoreType.DMA((14,)),
            pltpu.SemaphoreType.DMA((groups,)),
            pltpu.SemaphoreType.DMA,
            pltpu.SemaphoreType.DMA,
            pltpu.SemaphoreType.DMA,
            pltpu.SemaphoreType.DMA,
        ],
        compiler_params=pltpu.CompilerParams(
            collective_id=0, has_side_effects=True, vmem_limit_bytes=40 * 1024 * 1024
        ),
    )(*(pltpu.with_memory_space_constraint(x, pltpu.HBM) for x in operands))
    land_out, dust_out = pl.pallas_call(
        functools.partial(unpack, nblocks, half),
        out_shape=(
            jax.ShapeDtypeStruct((2 * nblocks, ncells), F32),
            jax.ShapeDtypeStruct((nbins * levels, columns), F32),
        ),
        in_specs=[pl.BlockSpec(memory_space=pltpu.VMEM)],
        out_specs=(pl.BlockSpec(memory_space=pltpu.HBM), pl.BlockSpec(memory_space=pltpu.HBM)),
        scratch_shapes=[pltpu.SemaphoreType.DMA((3,))],
        compiler_params=pltpu.CompilerParams(vmem_limit_bytes=16 * 1024 * 1024),
    )(pltpu.with_memory_space_constraint(results, pltpu.VMEM))
    return land_out.reshape(2, nblocks, ncells), dust_out.reshape(nbins, levels, columns)


def solution(mesh):
    both = ("sec", "tile")
    in_specs = (
        P(both, None),
        P(both, None),
        P(both, None),
        P(both, None),
        P(both),
        P(),
        P(),
        P(both, None),
        P(both, None, None),
        P(None, None, both),
        P(None, None, both),
        P(None, both),
        P(),
    )
    out_specs = (P(None, both, None), P(None, None, both))
    return jax.shard_map(
        functools.partial(on_device, mesh.shape["tile"]),
        mesh=mesh, in_specs=in_specs, out_specs=out_specs, check_vma=False,
    )
```

```python
import functools

import jax
import jax.numpy as jnp
import numpy as np
from jax import lax
from jax.experimental import pallas as pl
from jax.experimental.pallas import tpu as pltpu
from jax.sharding import PartitionSpec as P

FLAT = pl.DeviceIdType.LOGICAL
STEP = 4
GROUP = 16
F32 = jnp.float32
BF16 = jnp.bfloat16
FIXED = 65535.0


def threshold_constants(count):
    diameter = 4e-05 * np.power(1.35, np.arange(count))
    return np.sqrt(0.0123 * (2160.0 * 9.81 * diameter + 0.0003 / (1.227 * diameter)))


def rows_of(values, shape):
    row = lax.broadcasted_iota(jnp.int32, shape, 0)
    total = jnp.zeros(shape, F32)
    for r, value in enumerate(values):
        total = jnp.where(row == r, value, total)
    return total


def kernel(
    n, nt, nblocks, ncells, columns, nbins, nsalt, ntex, levels,
    wind_hbm, moist_hbm, tex_hbm, index_hbm, map_hbm, frac_hbm, blast_hbm, dest_hbm,
    w_hbm, atm_hbm, dust_hbm, mix_hbm, settle_hbm,
    results,
    wind, moist, tex, index, soil, frac, blast, dest_v, dest_s, w, atm, dust, mix, settle,
    packed, erod, root, coef, emitted, part, sums, send, came, mine, gath, numer, base, gain,
    in_sem, w_sem, surf_send, surf_recv, flux_send, flux_recv,
):
    half = columns // 2
    me = lax.axis_index("sec") * nt + lax.axis_index("tile")

    def local(src, dst, k):
        copy = pltpu.make_async_copy(src, dst, in_sem.at[k])
        copy.start()
        return copy

    copies = [
        local(src, dst, k)
        for k, (src, dst) in enumerate(
            [
                (map_hbm, soil), (index_hbm, index), (mix_hbm, mix), (atm_hbm, atm),
                (wind_hbm, wind), (moist_hbm, moist), (tex_hbm, tex), (frac_hbm, frac),
                (blast_hbm, blast), (dest_hbm, dest_v), (dest_hbm, dest_s), (settle_hbm, settle),
                (dust_hbm.at[:, 0:half], dust.at[0]), (dust_hbm.at[:, half:columns], dust.at[1]),
            ]
        )
    ]
    groups = nblocks // GROUP

    def chunk(i):
        at = pl.ds(i * GROUP, GROUP)
        return pltpu.make_async_copy(w_hbm.at[at], w.at[at], w_sem.at[i])

    for i in range(groups):
        chunk(i).start()

    def turned(i):
        p = me + i
        return jnp.where(p >= n, p - n, p)

    def each_peer(act):
        def several(i, carry):
            for j in range(STEP):
                one(i * STEP + j + 1)
            return carry

        def one(i):
            act(turned(i))

        lax.fori_loop(0, (n - 1) // STEP, several, 0)
        for i in range((n - 1) // STEP * STEP + 1, n):
            one(i)

    barrier = pltpu.get_barrier_semaphore()

    def greet(p):
        pl.semaphore_signal(barrier, inc=1, device_id=p, device_id_type=FLAT)

    each_peer(greet)

    for copy in copies[:10]:
        copy.wait()

    above = None
    held = [None] * 3
    for level in range(levels - 1, -1, -1):
        pivot = jnp.ones((1, columns), F32)
        low = up = None
        if level > 0:
            low = mix[level - 1:level, :]
            pivot = pivot + low
        if level < levels - 1:
            up = mix[level:level + 1, :]
            pivot = pivot + up * (1.0 - above)
        inverse = 1.0 / pivot
        for f in range(3):
            right = atm[f, level:level + 1, :]
            if up is not None:
                right = right + up * held[f]
            held[f] = right * inverse
        if low is not None:
            above = low * inverse
    speed = jnp.sqrt(held[0] * held[0] + held[1] * held[1] + 0.25)
    mine[0:1, :] = speed.astype(BF16).astype(F32)
    mine[1:2, :] = held[2].astype(BF16).astype(F32)

    words = soil.shape[0] // 2
    fixed = jnp.floor(soil[...] * FIXED + 0.5).astype(jnp.int32)
    packed[...] = fixed[:words] + (fixed[words:] << 16)
    bits = words.bit_length() - 1

    coef[...] = jnp.zeros_like(coef)
    for t in range(ntex):
        coef[:, 16 * t:16 * t + nsalt] = 40.0 * blast[t] * frac[t:t + 1, :]
    root[...] = jnp.sqrt(1.0 + 12.1 * moist[...])

    full = coef[:, 0:16 * ntex]
    coarse = full.astype(BF16)
    fine = (full - coarse.astype(F32)).astype(BF16)
    table = jnp.concatenate([coarse, fine], axis=0)
    thresh0 = rows_of([float(v) for v in threshold_constants(nsalt)], (16, ncells))
    nothing = jnp.zeros((nbins, ncells), F32)

    def erode(i):
        for j in range(GROUP // 8):
            erode_rows(i * (GROUP // 8) + j)

    def erode_rows(i):
        at = pl.ds(pl.multiple_of(i * 8, 8), 8)
        cell = index[at, :]
        lane = cell & 127
        row = cell >> 7
        picks = [((row >> b) & 1) == 1 for b in range(bits)]

        def tree(bit, first):
            if bit < 0:
                words_row = jnp.broadcast_to(packed[first:first + 1, :], (8, 128))
                return jnp.take_along_axis(words_row, lane, axis=1, mode="promise_in_bounds")
            return jnp.where(picks[bit], tree(bit - 1, first + (1 << bit)), tree(bit - 1, first))

        word = tree(bits - 1, 0)
        value = jnp.where(row >= words, lax.shift_right_logical(word, 16), word) & 65535
        erod[at, :] = value.astype(F32) * (1.0 / FIXED)

    def emit(i):
        blocks = []
        for j in range(GROUP):
            at = pl.ds(i * GROUP + j, 1)
            speed_row = jnp.broadcast_to(wind[at, :], (16, ncells))
            thresh = thresh0 * jnp.broadcast_to(root[at, :], (16, ncells))
            total = speed_row + thresh
            salt = jnp.broadcast_to(erod[at, :], (16, ncells)) * total * (
                total * jnp.maximum(speed_row - thresh, 0.0)
            )
            kind = jnp.broadcast_to(tex[at, :], (16, ncells))
            blocks.append(
                jnp.concatenate(
                    [jnp.where(kind == t, salt, 0.0).astype(BF16) for t in range(ntex)], axis=0
                )
            )
        both = jnp.dot(table, jnp.concatenate(blocks, axis=1), preferred_element_type=F32)
        emission = both[0:nbins] + both[nbins:2 * nbins]
        for j in range(0, GROUP, 2):
            first = emission[:, j * ncells:(j + 1) * ncells]
            second = emission[:, (j + 1) * ncells:(j + 2) * ncells]
            left = jnp.concatenate(
                [
                    jnp.concatenate([first, nothing], axis=1),
                    jnp.concatenate([nothing, second], axis=1),
                ],
                axis=0,
            )
            at = pl.ds(pl.multiple_of((i * (GROUP // 2) + j // 2) * 16, 16), 16)
            emitted[at, :] = left.astype(BF16)

    def regrid(i):
        for j in range(0, GROUP, 2):
            at = pl.ds(pl.multiple_of((i * (GROUP // 2) + j // 2) * 16, 16), 16)
            weights = w[pl.ds(i * GROUP + j, 2)].reshape(2 * ncells, columns)
            flux = jnp.dot(emitted[at, :], weights, preferred_element_type=F32)
            for s in range(2):
                at = pl.ds(i * GROUP + j + s, nbins, stride=nblocks)
                part[0, at, :] = flux[s * nbins:(s + 1) * nbins, 0:half]
                part[1, at, :] = flux[s * nbins:(s + 1) * nbins, half:columns]

    erode(0)
    emit(0)
    erode(1)

    pl.semaphore_wait(barrier, n - 1)

    def send_surface(p):
        pltpu.make_async_remote_copy(
            src_ref=mine, dst_ref=gath.at[me], send_sem=surf_send, recv_sem=surf_recv,
            device_id=p, device_id_type=FLAT,
        ).start()

    gath[me] = mine[...]
    share = (n - 1) // (groups - 2)
    for i in range(share * (groups - 2) + 1, n):
        send_surface(turned(i))

    def steps(i, carry):
        for j in range(share):
            send_surface(turned((i - 2) * share + j + 1))
        chunk(i - 2).wait()
        regrid(i - 2)
        emit(i - 1)
        erode(i)
        return carry

    lax.fori_loop(2, groups, steps, 0)
    chunk(groups - 2).wait()
    chunk(groups - 1).wait()
    regrid(groups - 2)
    emit(groups - 1)
    regrid(groups - 1)

    tiles = lax.broadcasted_iota(jnp.int32, (n, nblocks), 0)
    placing = jnp.where(jnp.broadcast_to(dest_v[...], (n, nblocks)) == tiles, 1.0, 0.0).astype(BF16)
    placing = jnp.concatenate([placing, placing], axis=1)
    for k in range(nbins):
        at = slice(k * nblocks, (k + 1) * nblocks)
        block = jnp.concatenate([part[0, at, :], part[1, at, :]], axis=1)
        high = block.astype(BF16)
        low = (block - high.astype(F32)).astype(BF16)
        total = jnp.dot(placing, jnp.concatenate([high, low], axis=0), preferred_element_type=F32)
        sums[pl.ds(k, n, stride=2 * nbins), :] = total[:, 0:half]
        sums[pl.ds(nbins + k, n, stride=2 * nbins), :] = total[:, half:columns]
    send[...] = sums[...].reshape(n, 2 * nbins, half).astype(BF16)

    def send_flux(p):
        pltpu.make_async_remote_copy(
            src_ref=send.at[p], dst_ref=came.at[me], send_sem=flux_send, recv_sem=flux_recv,
            device_id=p, device_id_type=FLAT,
        ).start()

    each_peer(send_flux)
    came[me] = send[me]

    for copy in copies[10:]:
        copy.wait()
    sink = rows_of([settle[0, f] for f in range(nbins)], (nbins, columns))
    ratios = [None] * levels
    values = [None] * levels
    for level in range(levels - 1, -1, -1):
        pivot = jnp.ones((nbins, columns), F32)
        at = pl.ds(level, nbins, stride=levels)
        right = jnp.concatenate([dust[0, at, :], dust[1, at, :]], axis=1)
        low = None
        if level > 0:
            low = jnp.broadcast_to(mix[level - 1:level, :], (nbins, columns))
            pivot = pivot + low
        if level < levels - 1:
            up = jnp.broadcast_to(mix[level:level + 1, :], (nbins, columns)) + sink
            pivot = pivot + up * (1.0 - ratios[level + 1])
            right = right + up * values[level + 1]
        else:
            pivot = pivot + sink
        inverse = 1.0 / pivot
        values[level] = right * inverse
        if low is not None:
            ratios[level] = low * inverse
    scale = float(columns) / float(ncells * nblocks)
    now, step = values[0], inverse * scale
    base[0], gain[0] = now, step
    for level in range(1, levels):
        now = values[level] + ratios[level] * now
        step = ratios[level] * step
        base[level], gain[level] = now, step

    arrived = gath.at[pl.ds(0, n - 1)]
    pltpu.make_async_copy(arrived, arrived, surf_recv).wait()
    rest = jnp.where(lax.broadcasted_iota(jnp.int32, (6, columns), 0) == 0, 1.0, 0.0)

    def back(i, carry):
        for j in range(0, GROUP, 2):
            g = i * GROUP + j
            left = jnp.concatenate(
                [gath[dest_s[0, g]], rest, gath[dest_s[0, g + 1]], rest], axis=0
            ).astype(BF16)
            weights = w[pl.ds(g, 2)].reshape(2 * ncells, columns)
            found = lax.dot_general(
                left, weights, (((1,), (1,)), ((), ())), preferred_element_type=F32
            )
            numer[pl.ds(pl.multiple_of(g * 8, 8), 8), :] = found[0:8, 0:ncells]
            numer[pl.ds(pl.multiple_of(g * 8 + 8, 8), 8), :] = found[8:16, ncells:2 * ncells]
        return carry

    lax.fori_loop(0, groups, back, 0)
    weight = 1.0 / numer[pl.ds(2, nblocks, stride=8), :]
    results[0:nblocks, :] = numer[pl.ds(0, nblocks, stride=8), :] * weight
    results[nblocks:2 * nblocks, :] = 0.5 * moist[...] + 0.5 * (numer[pl.ds(1, nblocks, stride=8), :] * weight)

    landed = came.at[pl.ds(0, n - 1)]
    pltpu.make_async_copy(landed, landed, flux_recv).wait()
    flux = jnp.sum(came[...].astype(F32), axis=0)
    flux = jnp.concatenate([flux[0:nbins], flux[nbins:2 * nbins]], axis=1)
    for level in range(levels):
        total = base[level] + gain[level] * flux
        for h in range(2):
            first = 2 * nblocks + h * nbins * levels + level
            results[pl.ds(first, nbins, stride=levels), :] = total[:, h * half:(h + 1) * half]

    sent = gath.at[pl.ds(0, n - 1)]
    pltpu.make_async_copy(sent, sent, surf_send).wait()
    gone = came.at[pl.ds(0, n - 1)]
    pltpu.make_async_copy(gone, gone, flux_send).wait()


def unpack(nblocks, half, results, land_out, dust_out, sem):
    rows = dust_out.shape[0]
    copies = [
        pltpu.make_async_copy(results.at[pl.ds(0, 2 * nblocks)], land_out, sem.at[0]),
        pltpu.make_async_copy(
            results.at[pl.ds(2 * nblocks, rows)], dust_out.at[:, 0:half], sem.at[1]
        ),
        pltpu.make_async_copy(
            results.at[pl.ds(2 * nblocks + rows, rows)], dust_out.at[:, half:2 * half], sem.at[2]
        ),
    ]
    for copy in copies:
        copy.start()
    for copy in copies:
        copy.wait()


def on_device(
    nt, land_wind, land_moist, texture, land_index, erod_map, mass_frac, blast_table, dest_tile,
    regrid_w, atm_state, dust_mix, mixing, settle,
):
    nblocks, ncells = land_wind.shape
    columns = regrid_w.shape[2]
    ntex, nbins, nsalt = blast_table.shape
    levels = atm_state.shape[1]
    half = columns // 2
    n = lax.axis_size(("sec", "tile"))
    groups = nblocks // GROUP
    soil = erod_map.reshape(-1, 128)
    operands = (
        land_wind, land_moist, texture, land_index, soil, mass_frac, blast_table,
        dest_tile.reshape(1, nblocks), regrid_w, atm_state,
        dust_mix.reshape(nbins * levels, columns), mixing, settle.reshape(1, nbins),
    )
    land = pltpu.VMEM((nblocks, ncells), F32)
    whole = pltpu.VMEM((nblocks, ncells), jnp.int32)
    results = pl.pallas_call(
        functools.partial(kernel, n, nt, nblocks, ncells, columns, nbins, nsalt, ntex, levels),
        out_shape=jax.ShapeDtypeStruct((2 * nblocks + 2 * nbins * levels, 128), F32),
        in_specs=[pl.BlockSpec(memory_space=pltpu.HBM)] * 13,
        out_specs=pl.BlockSpec(memory_space=pltpu.VMEM),
        scratch_shapes=[
            land,
            land,
            whole,
            whole,
            pltpu.VMEM(soil.shape, F32),
            pltpu.VMEM(mass_frac.shape, F32),
            pltpu.VMEM(blast_table.shape, F32),
            pltpu.VMEM((1, nblocks), jnp.int32),
            pltpu.SMEM((1, nblocks), jnp.int32),
            pltpu.VMEM(regrid_w.shape, BF16),
            pltpu.VMEM(atm_state.shape, F32),
            pltpu.VMEM((2, nbins * levels, half), F32),
            pltpu.VMEM(mixing.shape, F32),
            pltpu.SMEM((1, nbins), F32),
            pltpu.VMEM((soil.shape[0] // 2, 128), jnp.int32),
            land,
            land,
            pltpu.VMEM((nbins, 128), F32),
            pltpu.VMEM((nblocks * nbins, columns), BF16),
            pltpu.VMEM((2, nbins * nblocks, half), F32),
            pltpu.VMEM((n * 2 * nbins, half), F32),
            pltpu.VMEM((n, 2 * nbins, half), BF16),
            pltpu.VMEM((n, 2 * nbins, half), BF16),
            pltpu.VMEM((2, columns), F32),
            pltpu.VMEM((n, 2, columns), F32),
            pltpu.VMEM((nblocks * 8, ncells), F32),
            pltpu.VMEM((levels, nbins, columns), F32),
            pltpu.VMEM((levels, nbins, columns), F32),
            pltpu.SemaphoreType.DMA((14,)),
            pltpu.SemaphoreType.DMA((groups,)),
            pltpu.SemaphoreType.DMA,
            pltpu.SemaphoreType.DMA,
            pltpu.SemaphoreType.DMA,
            pltpu.SemaphoreType.DMA,
        ],
        compiler_params=pltpu.CompilerParams(
            collective_id=0, has_side_effects=True, vmem_limit_bytes=40 * 1024 * 1024
        ),
    )(*(pltpu.with_memory_space_constraint(x, pltpu.HBM) for x in operands))
    land_out, dust_out = pl.pallas_call(
        functools.partial(unpack, nblocks, half),
        out_shape=(
            jax.ShapeDtypeStruct((2 * nblocks, ncells), F32),
            jax.ShapeDtypeStruct((nbins * levels, columns), F32),
        ),
        in_specs=[pl.BlockSpec(memory_space=pltpu.VMEM)],
        out_specs=(pl.BlockSpec(memory_space=pltpu.HBM), pl.BlockSpec(memory_space=pltpu.HBM)),
        scratch_shapes=[pltpu.SemaphoreType.DMA((3,))],
        compiler_params=pltpu.CompilerParams(vmem_limit_bytes=16 * 1024 * 1024),
    )(pltpu.with_memory_space_constraint(results, pltpu.VMEM))
    return land_out.reshape(2, nblocks, ncells), dust_out.reshape(nbins, levels, columns)


def solution(mesh):
    both = ("sec", "tile")
    in_specs = (
        P(both, None),
        P(both, None),
        P(both, None),
        P(both, None),
        P(both),
        P(),
        P(),
        P(both, None),
        P(both, None, None),
        P(None, None, both),
        P(None, None, both),
        P(None, both),
        P(),
    )
    out_specs = (P(None, both, None), P(None, None, both))
    return jax.shard_map(
        functools.partial(on_device, mesh.shape["tile"]),
        mesh=mesh, in_specs=in_specs, out_specs=out_specs, check_vma=False,
    )
```

```python
import functools

import jax
import jax.numpy as jnp
import numpy as np
from jax import lax
from jax.experimental import pallas as pl
from jax.experimental.pallas import tpu as pltpu
from jax.sharding import PartitionSpec as P

FLAT = pl.DeviceIdType.LOGICAL
STEP = 4
GROUP = 16
F32 = jnp.float32
BF16 = jnp.bfloat16
FIXED = 65535.0


def threshold_constants(count):
    diameter = 4e-05 * np.power(1.35, np.arange(count))
    return np.sqrt(0.0123 * (2160.0 * 9.81 * diameter + 0.0003 / (1.227 * diameter)))


def rows_of(values, shape):
    row = lax.broadcasted_iota(jnp.int32, shape, 0)
    total = jnp.zeros(shape, F32)
    for r, value in enumerate(values):
        total = jnp.where(row == r, value, total)
    return total


def kernel(
    n, nt, nblocks, ncells, columns, nbins, nsalt, ntex, levels,
    wind_hbm, moist_hbm, tex_hbm, index_hbm, map_hbm, frac_hbm, blast_hbm, dest_hbm,
    w_hbm, atm_hbm, dust_hbm, mix_hbm, settle_hbm,
    results,
    wind, moist, tex, index, soil, frac, blast, dest_v, dest_s, w, atm, dust, mix, settle,
    packed, erod, root, coef, emitted, part, sums, send, came, mine, gath, picked, numer, base, gain,
    in_sem, w_sem, surf_send, surf_recv, flux_send, flux_recv,
):
    half = columns // 2
    me = lax.axis_index("sec") * nt + lax.axis_index("tile")

    def local(src, dst, k):
        copy = pltpu.make_async_copy(src, dst, in_sem.at[k])
        copy.start()
        return copy

    copies = [
        local(src, dst, k)
        for k, (src, dst) in enumerate(
            [
                (map_hbm, soil), (index_hbm, index), (mix_hbm, mix), (atm_hbm, atm),
                (wind_hbm, wind), (moist_hbm, moist), (tex_hbm, tex), (frac_hbm, frac),
                (blast_hbm, blast), (dest_hbm, dest_v), (dest_hbm, dest_s), (settle_hbm, settle),
                (dust_hbm.at[:, 0:half], dust.at[0]), (dust_hbm.at[:, half:columns], dust.at[1]),
            ]
        )
    ]
    groups = nblocks // GROUP

    def chunk(i):
        at = pl.ds(i * GROUP, GROUP)
        return pltpu.make_async_copy(w_hbm.at[at], w.at[at], w_sem.at[i])

    for i in range(groups):
        chunk(i).start()

    def turned(i):
        p = me + i
        return jnp.where(p >= n, p - n, p)

    def each_peer(act):
        def several(i, carry):
            for j in range(STEP):
                one(i * STEP + j + 1)
            return carry

        def one(i):
            act(turned(i))

        lax.fori_loop(0, (n - 1) // STEP, several, 0)
        for i in range((n - 1) // STEP * STEP + 1, n):
            one(i)

    barrier = pltpu.get_barrier_semaphore()

    def greet(p):
        pl.semaphore_signal(barrier, inc=1, device_id=p, device_id_type=FLAT)

    each_peer(greet)

    for copy in copies[:10]:
        copy.wait()

    above = None
    held = [None] * 3
    for level in range(levels - 1, -1, -1):
        pivot = jnp.ones((1, columns), F32)
        low = up = None
        if level > 0:
            low = mix[level - 1:level, :]
            pivot = pivot + low
        if level < levels - 1:
            up = mix[level:level + 1, :]
            pivot = pivot + up * (1.0 - above)
        inverse = 1.0 / pivot
        for f in range(3):
            right = atm[f, level:level + 1, :]
            if up is not None:
                right = right + up * held[f]
            held[f] = right * inverse
        if low is not None:
            above = low * inverse
    speed = jnp.sqrt(held[0] * held[0] + held[1] * held[1] + 0.25)
    mine[0:1, :] = speed.astype(BF16).astype(F32)
    mine[1:2, :] = held[2].astype(BF16).astype(F32)

    words = soil.shape[0] // 2
    fixed = jnp.floor(soil[...] * FIXED + 0.5).astype(jnp.int32)
    packed[...] = fixed[:words] + (fixed[words:] << 16)
    bits = words.bit_length() - 1

    coef[...] = jnp.zeros_like(coef)
    for t in range(ntex):
        coef[:, 16 * t:16 * t + nsalt] = 40.0 * blast[t] * frac[t:t + 1, :]
    root[...] = jnp.sqrt(1.0 + 12.1 * moist[...])

    full = coef[:, 0:16 * ntex]
    coarse = full.astype(BF16)
    fine = (full - coarse.astype(F32)).astype(BF16)
    table = jnp.concatenate([coarse, fine], axis=0)
    thresh0 = rows_of([float(v) for v in threshold_constants(nsalt)], (16, ncells))
    nothing = jnp.zeros((nbins, ncells), F32)

    def erode(i):
        for j in range(GROUP // 8):
            erode_rows(i * (GROUP // 8) + j)

    def erode_rows(i):
        at = pl.ds(pl.multiple_of(i * 8, 8), 8)
        cell = index[at, :]
        lane = cell & 127
        row = cell >> 7
        picks = [((row >> b) & 1) == 1 for b in range(bits)]

        def tree(bit, first):
            if bit < 0:
                words_row = jnp.broadcast_to(packed[first:first + 1, :], (8, 128))
                return jnp.take_along_axis(words_row, lane, axis=1, mode="promise_in_bounds")
            return jnp.where(picks[bit], tree(bit - 1, first + (1 << bit)), tree(bit - 1, first))

        word = tree(bits - 1, 0)
        value = jnp.where(row >= words, lax.shift_right_logical(word, 16), word) & 65535
        erod[at, :] = value.astype(F32) * (1.0 / FIXED)

    def emit(i):
        blocks = []
        for j in range(GROUP):
            at = pl.ds(i * GROUP + j, 1)
            speed_row = jnp.broadcast_to(wind[at, :], (16, ncells))
            thresh = thresh0 * jnp.broadcast_to(root[at, :], (16, ncells))
            total = speed_row + thresh
            salt = jnp.broadcast_to(erod[at, :], (16, ncells)) * total * (
                total * jnp.maximum(speed_row - thresh, 0.0)
            )
            kind = jnp.broadcast_to(tex[at, :], (16, ncells))
            blocks.append(
                jnp.concatenate(
                    [jnp.where(kind == t, salt, 0.0).astype(BF16) for t in range(ntex)], axis=0
                )
            )
        both = jnp.dot(table, jnp.concatenate(blocks, axis=1), preferred_element_type=F32)
        emission = both[0:nbins] + both[nbins:2 * nbins]
        for j in range(0, GROUP, 2):
            first = emission[:, j * ncells:(j + 1) * ncells]
            second = emission[:, (j + 1) * ncells:(j + 2) * ncells]
            left = jnp.concatenate(
                [
                    jnp.concatenate([first, nothing], axis=1),
                    jnp.concatenate([nothing, second], axis=1),
                ],
                axis=0,
            )
            at = pl.ds(pl.multiple_of((i * (GROUP // 2) + j // 2) * 16, 16), 16)
            emitted[at, :] = left.astype(BF16)

    def regrid(i):
        for j in range(0, GROUP, 2):
            at = pl.ds(pl.multiple_of((i * (GROUP // 2) + j // 2) * 16, 16), 16)
            weights = w[pl.ds(i * GROUP + j, 2)].reshape(2 * ncells, columns)
            flux = jnp.dot(emitted[at, :], weights, preferred_element_type=F32)
            for s in range(2):
                at = pl.ds(i * GROUP + j + s, nbins, stride=nblocks)
                part[0, at, :] = flux[s * nbins:(s + 1) * nbins, 0:half]
                part[1, at, :] = flux[s * nbins:(s + 1) * nbins, half:columns]

    erode(0)
    emit(0)
    erode(1)

    pl.semaphore_wait(barrier, n - 1)

    def send_surface(p):
        pltpu.make_async_remote_copy(
            src_ref=mine, dst_ref=gath.at[me], send_sem=surf_send, recv_sem=surf_recv,
            device_id=p, device_id_type=FLAT,
        ).start()

    gath[me] = mine[...]
    share = (n - 1) // (groups - 2)
    for i in range(share * (groups - 2) + 1, n):
        send_surface(turned(i))

    def steps(i, carry):
        for j in range(share):
            send_surface(turned((i - 2) * share + j + 1))
        chunk(i - 2).wait()
        regrid(i - 2)
        emit(i - 1)
        erode(i)
        return carry

    lax.fori_loop(2, groups, steps, 0)
    chunk(groups - 2).wait()
    chunk(groups - 1).wait()
    regrid(groups - 2)
    emit(groups - 1)
    regrid(groups - 1)

    tiles = lax.broadcasted_iota(jnp.int32, (n, nblocks), 0)
    placing = jnp.where(jnp.broadcast_to(dest_v[...], (n, nblocks)) == tiles, 1.0, 0.0).astype(BF16)
    placing = jnp.concatenate([placing, placing], axis=1)
    for k in range(nbins):
        at = slice(k * nblocks, (k + 1) * nblocks)
        block = jnp.concatenate([part[0, at, :], part[1, at, :]], axis=1)
        high = block.astype(BF16)
        low = (block - high.astype(F32)).astype(BF16)
        total = jnp.dot(placing, jnp.concatenate([high, low], axis=0), preferred_element_type=F32)
        sums[pl.ds(k, n, stride=2 * nbins), :] = total[:, 0:half]
        sums[pl.ds(nbins + k, n, stride=2 * nbins), :] = total[:, half:columns]
    send[...] = sums[...].reshape(n, 2 * nbins, half).astype(BF16)

    def send_flux(p):
        pltpu.make_async_remote_copy(
            src_ref=send.at[p], dst_ref=came.at[me], send_sem=flux_send, recv_sem=flux_recv,
            device_id=p, device_id_type=FLAT,
        ).start()

    each_peer(send_flux)
    came[me] = send[me]

    for copy in copies[10:]:
        copy.wait()
    sink = rows_of([settle[0, f] for f in range(nbins)], (nbins, columns))
    ratios = [None] * levels
    values = [None] * levels
    for level in range(levels - 1, -1, -1):
        pivot = jnp.ones((nbins, columns), F32)
        at = pl.ds(level, nbins, stride=levels)
        right = jnp.concatenate([dust[0, at, :], dust[1, at, :]], axis=1)
        low = None
        if level > 0:
            low = jnp.broadcast_to(mix[level - 1:level, :], (nbins, columns))
            pivot = pivot + low
        if level < levels - 1:
            up = jnp.broadcast_to(mix[level:level + 1, :], (nbins, columns)) + sink
            pivot = pivot + up * (1.0 - ratios[level + 1])
            right = right + up * values[level + 1]
        else:
            pivot = pivot + sink
        inverse = 1.0 / pivot
        values[level] = right * inverse
        if low is not None:
            ratios[level] = low * inverse
    scale = float(columns) / float(ncells * nblocks)
    now, step = values[0], inverse * scale
    base[0], gain[0] = now, step
    for level in range(1, levels):
        now = values[level] + ratios[level] * now
        step = ratios[level] * step
        base[level], gain[level] = now, step

    arrived = gath.at[pl.ds(0, n - 1)]
    pltpu.make_async_copy(arrived, arrived, surf_recv).wait()
    picked[...] = jnp.where(
        lax.broadcasted_iota(jnp.int32, picked.shape, 0) % 4 == 2, 1.0, 0.0
    )
    owner = lax.broadcasted_iota(jnp.int32, (ncells, 128), 1) // 4

    def back(q, carry):
        for j in range(32):
            picked[4 * j:4 * j + 2, :] = gath[dest_s[0, q * 32 + j]]
        across = picked[...].T.astype(BF16)
        found = jnp.zeros((ncells, 128), F32)
        for j in range(0, 32, 8):
            rows = w[pl.ds(q * 32 + j, 8)].reshape(8 * ncells, columns)
            product = jnp.dot(rows, across, preferred_element_type=F32)
            for s in range(8):
                found = jnp.where(owner == j + s, product[s * ncells:(s + 1) * ncells], found)
        numer[pl.ds(pl.multiple_of(q * 128, 128), 128), :] = found.T
        return carry

    lax.fori_loop(0, nblocks // 32, back, 0)
    weight = 1.0 / numer[pl.ds(2, nblocks, stride=4), :]
    results[0:nblocks, :] = numer[pl.ds(0, nblocks, stride=4), :] * weight
    results[nblocks:2 * nblocks, :] = (
        0.5 * moist[...] + 0.5 * (numer[pl.ds(1, nblocks, stride=4), :] * weight)
    )

    landed = came.at[pl.ds(0, n - 1)]
    pltpu.make_async_copy(landed, landed, flux_recv).wait()
    flux = jnp.sum(came[...].astype(F32), axis=0)
    flux = jnp.concatenate([flux[0:nbins], flux[nbins:2 * nbins]], axis=1)
    for level in range(levels):
        total = base[level] + gain[level] * flux
        for h in range(2):
            first = 2 * nblocks + h * nbins * levels + level
            results[pl.ds(first, nbins, stride=levels), :] = total[:, h * half:(h + 1) * half]

    sent = gath.at[pl.ds(0, n - 1)]
    pltpu.make_async_copy(sent, sent, surf_send).wait()
    gone = came.at[pl.ds(0, n - 1)]
    pltpu.make_async_copy(gone, gone, flux_send).wait()


def unpack(nblocks, half, results, land_out, dust_out, sem):
    rows = dust_out.shape[0]
    copies = [
        pltpu.make_async_copy(results.at[pl.ds(0, 2 * nblocks)], land_out, sem.at[0]),
        pltpu.make_async_copy(
            results.at[pl.ds(2 * nblocks, rows)], dust_out.at[:, 0:half], sem.at[1]
        ),
        pltpu.make_async_copy(
            results.at[pl.ds(2 * nblocks + rows, rows)], dust_out.at[:, half:2 * half], sem.at[2]
        ),
    ]
    for copy in copies:
        copy.start()
    for copy in copies:
        copy.wait()


def on_device(
    nt, land_wind, land_moist, texture, land_index, erod_map, mass_frac, blast_table, dest_tile,
    regrid_w, atm_state, dust_mix, mixing, settle,
):
    nblocks, ncells = land_wind.shape
    columns = regrid_w.shape[2]
    ntex, nbins, nsalt = blast_table.shape
    levels = atm_state.shape[1]
    half = columns // 2
    n = lax.axis_size(("sec", "tile"))
    groups = nblocks // GROUP
    soil = erod_map.reshape(-1, 128)
    operands = (
        land_wind, land_moist, texture, land_index, soil, mass_frac, blast_table,
        dest_tile.reshape(1, nblocks), regrid_w, atm_state,
        dust_mix.reshape(nbins * levels, columns), mixing, settle.reshape(1, nbins),
    )
    land = pltpu.VMEM((nblocks, ncells), F32)
    whole = pltpu.VMEM((nblocks, ncells), jnp.int32)
    results = pl.pallas_call(
        functools.partial(kernel, n, nt, nblocks, ncells, columns, nbins, nsalt, ntex, levels),
        out_shape=jax.ShapeDtypeStruct((2 * nblocks + 2 * nbins * levels, 128), F32),
        in_specs=[pl.BlockSpec(memory_space=pltpu.HBM)] * 13,
        out_specs=pl.BlockSpec(memory_space=pltpu.VMEM),
        scratch_shapes=[
            land,
            land,
            whole,
            whole,
            pltpu.VMEM(soil.shape, F32),
            pltpu.VMEM(mass_frac.shape, F32),
            pltpu.VMEM(blast_table.shape, F32),
            pltpu.VMEM((1, nblocks), jnp.int32),
            pltpu.SMEM((1, nblocks), jnp.int32),
            pltpu.VMEM(regrid_w.shape, BF16),
            pltpu.VMEM(atm_state.shape, F32),
            pltpu.VMEM((2, nbins * levels, half), F32),
            pltpu.VMEM(mixing.shape, F32),
            pltpu.SMEM((1, nbins), F32),
            pltpu.VMEM((soil.shape[0] // 2, 128), jnp.int32),
            land,
            land,
            pltpu.VMEM((nbins, 128), F32),
            pltpu.VMEM((nblocks * nbins, columns), BF16),
            pltpu.VMEM((2, nbins * nblocks, half), F32),
            pltpu.VMEM((n * 2 * nbins, half), F32),
            pltpu.VMEM((n, 2 * nbins, half), BF16),
            pltpu.VMEM((n, 2 * nbins, half), BF16),
            pltpu.VMEM((2, columns), F32),
            pltpu.VMEM((n, 2, columns), F32),
            pltpu.VMEM((128, columns), F32),
            pltpu.VMEM((nblocks * 4, ncells), F32),
            pltpu.VMEM((levels, nbins, columns), F32),
            pltpu.VMEM((levels, nbins, columns), F32),
            pltpu.SemaphoreType.DMA((14,)),
            pltpu.SemaphoreType.DMA((groups,)),
            pltpu.SemaphoreType.DMA,
            pltpu.SemaphoreType.DMA,
            pltpu.SemaphoreType.DMA,
            pltpu.SemaphoreType.DMA,
        ],
        compiler_params=pltpu.CompilerParams(
            collective_id=0, has_side_effects=True, vmem_limit_bytes=40 * 1024 * 1024
        ),
    )(*(pltpu.with_memory_space_constraint(x, pltpu.HBM) for x in operands))
    land_out, dust_out = pl.pallas_call(
        functools.partial(unpack, nblocks, half),
        out_shape=(
            jax.ShapeDtypeStruct((2 * nblocks, ncells), F32),
            jax.ShapeDtypeStruct((nbins * levels, columns), F32),
        ),
        in_specs=[pl.BlockSpec(memory_space=pltpu.VMEM)],
        out_specs=(pl.BlockSpec(memory_space=pltpu.HBM), pl.BlockSpec(memory_space=pltpu.HBM)),
        scratch_shapes=[pltpu.SemaphoreType.DMA((3,))],
        compiler_params=pltpu.CompilerParams(vmem_limit_bytes=16 * 1024 * 1024),
    )(pltpu.with_memory_space_constraint(results, pltpu.VMEM))
    return land_out.reshape(2, nblocks, ncells), dust_out.reshape(nbins, levels, columns)


def solution(mesh):
    both = ("sec", "tile")
    in_specs = (
        P(both, None),
        P(both, None),
        P(both, None),
        P(both, None),
        P(both),
        P(),
        P(),
        P(both, None),
        P(both, None, None),
        P(None, None, both),
        P(None, None, both),
        P(None, both),
        P(),
    )
    out_specs = (P(None, both, None), P(None, None, both))
    return jax.shard_map(
        functools.partial(on_device, mesh.shape["tile"]),
        mesh=mesh, in_specs=in_specs, out_specs=out_specs, check_vma=False,
    )
```

```python
import functools

import jax
import jax.numpy as jnp
import numpy as np
from jax import lax
from jax.experimental import pallas as pl
from jax.experimental.pallas import tpu as pltpu
from jax.sharding import PartitionSpec as P

FLAT = pl.DeviceIdType.LOGICAL
STEP = 4
GROUP = 16
F32 = jnp.float32
BF16 = jnp.bfloat16
FIXED = 65535.0


def threshold_constants(count):
    diameter = 4e-05 * np.power(1.35, np.arange(count))
    return np.sqrt(0.0123 * (2160.0 * 9.81 * diameter + 0.0003 / (1.227 * diameter)))


def rows_of(values, shape):
    row = lax.broadcasted_iota(jnp.int32, shape, 0)
    total = jnp.zeros(shape, F32)
    for r, value in enumerate(values):
        total = jnp.where(row == r, value, total)
    return total


def kernel(
    n, nt, nblocks, ncells, columns, nbins, nsalt, ntex, levels,
    wind_hbm, moist_hbm, tex_hbm, index_hbm, map_hbm, frac_hbm, blast_hbm, dest_hbm,
    w_hbm, atm_hbm, dust_hbm, mix_hbm, settle_hbm,
    results,
    wind, moist, tex, index, soil, frac, blast, dest_v, dest_s, w, atm, dust, mix, settle,
    packed, erod, root, coef, emitted, part, sums, send, came, mine, gath, numer, base, gain,
    in_sem, w_sem, surf_send, surf_recv, flux_send, flux_recv,
):
    half = columns // 2
    me = lax.axis_index("sec") * nt + lax.axis_index("tile")

    def local(src, dst, k):
        copy = pltpu.make_async_copy(src, dst, in_sem.at[k])
        copy.start()
        return copy

    copies = [
        local(src, dst, k)
        for k, (src, dst) in enumerate(
            [
                (map_hbm, soil), (index_hbm, index), (mix_hbm, mix), (atm_hbm, atm),
                (wind_hbm, wind), (moist_hbm, moist), (tex_hbm, tex), (frac_hbm, frac),
                (blast_hbm, blast), (dest_hbm, dest_v), (dest_hbm, dest_s), (settle_hbm, settle),
                (dust_hbm.at[:, 0:half], dust.at[0]), (dust_hbm.at[:, half:columns], dust.at[1]),
            ]
        )
    ]
    groups = nblocks // GROUP

    def chunk(i):
        at = pl.ds(i * GROUP, GROUP)
        return pltpu.make_async_copy(w_hbm.at[at], w.at[at], w_sem.at[i])

    for i in range(groups):
        chunk(i).start()

    def turned(i):
        p = me + i
        return jnp.where(p >= n, p - n, p)

    def each_peer(act):
        def several(i, carry):
            for j in range(STEP):
                one(i * STEP + j + 1)
            return carry

        def one(i):
            act(turned(i))

        lax.fori_loop(0, (n - 1) // STEP, several, 0)
        for i in range((n - 1) // STEP * STEP + 1, n):
            one(i)

    barrier = pltpu.get_barrier_semaphore()

    def greet(p):
        pl.semaphore_signal(barrier, inc=1, device_id=p, device_id_type=FLAT)

    each_peer(greet)

    for copy in copies[:10]:
        copy.wait()

    above = None
    held = [None] * 3
    for level in range(levels - 1, -1, -1):
        pivot = jnp.ones((1, columns), F32)
        low = up = None
        if level > 0:
            low = mix[level - 1:level, :]
            pivot = pivot + low
        if level < levels - 1:
            up = mix[level:level + 1, :]
            pivot = pivot + up * (1.0 - above)
        inverse = 1.0 / pivot
        for f in range(3):
            right = atm[f, level:level + 1, :]
            if up is not None:
                right = right + up * held[f]
            held[f] = right * inverse
        if low is not None:
            above = low * inverse
    speed = jnp.sqrt(held[0] * held[0] + held[1] * held[1] + 0.25)
    mine[0:1, :] = speed.astype(BF16).astype(F32)
    mine[1:2, :] = held[2].astype(BF16).astype(F32)

    words = soil.shape[0] // 2
    fixed = jnp.floor(soil[...] * FIXED + 0.5).astype(jnp.int32)
    packed[...] = fixed[:words] + (fixed[words:] << 16)
    bits = words.bit_length() - 1

    coef[...] = jnp.zeros_like(coef)
    for t in range(ntex):
        coef[:, 16 * t:16 * t + nsalt] = 40.0 * blast[t] * frac[t:t + 1, :]
    root[...] = jnp.sqrt(1.0 + 12.1 * moist[...])

    full = coef[:, 0:16 * ntex]
    coarse = full.astype(BF16)
    fine = (full - coarse.astype(F32)).astype(BF16)
    table = jnp.concatenate([coarse, fine], axis=0)
    thresh0 = rows_of([float(v) for v in threshold_constants(nsalt)], (16, ncells))
    nothing = jnp.zeros((nbins, ncells), F32)

    def erode(i):
        for j in range(GROUP // 8):
            erode_rows(i * (GROUP // 8) + j)

    def erode_rows(i):
        at = pl.ds(pl.multiple_of(i * 8, 8), 8)
        cell = index[at, :]
        lane = cell & 127
        row = cell >> 7
        picks = [((row >> b) & 1) == 1 for b in range(bits)]

        def tree(bit, first):
            if bit < 0:
                words_row = jnp.broadcast_to(packed[first:first + 1, :], (8, 128))
                return jnp.take_along_axis(words_row, lane, axis=1, mode="promise_in_bounds")
            return jnp.where(picks[bit], tree(bit - 1, first + (1 << bit)), tree(bit - 1, first))

        word = tree(bits - 1, 0)
        value = jnp.where(row >= words, lax.shift_right_logical(word, 16), word) & 65535
        erod[at, :] = value.astype(F32) * (1.0 / FIXED)

    def emit(i):
        blocks = []
        for j in range(GROUP):
            at = pl.ds(i * GROUP + j, 1)
            speed_row = jnp.broadcast_to(wind[at, :], (16, ncells))
            thresh = thresh0 * jnp.broadcast_to(root[at, :], (16, ncells))
            total = speed_row + thresh
            salt = jnp.broadcast_to(erod[at, :], (16, ncells)) * total * (
                total * jnp.maximum(speed_row - thresh, 0.0)
            )
            kind = jnp.broadcast_to(tex[at, :], (16, ncells))
            blocks.append(
                jnp.concatenate(
                    [jnp.where(kind == t, salt, 0.0).astype(BF16) for t in range(ntex)], axis=0
                )
            )
        both = jnp.dot(table, jnp.concatenate(blocks, axis=1), preferred_element_type=F32)
        emission = both[0:nbins] + both[nbins:2 * nbins]
        for j in range(0, GROUP, 2):
            first = emission[:, j * ncells:(j + 1) * ncells]
            second = emission[:, (j + 1) * ncells:(j + 2) * ncells]
            left = jnp.concatenate(
                [
                    jnp.concatenate([first, nothing], axis=1),
                    jnp.concatenate([nothing, second], axis=1),
                ],
                axis=0,
            )
            at = pl.ds(pl.multiple_of((i * (GROUP // 2) + j // 2) * 16, 16), 16)
            emitted[at, :] = left.astype(BF16)

    def regrid(i):
        for j in range(0, GROUP, 2):
            at = pl.ds(pl.multiple_of((i * (GROUP // 2) + j // 2) * 16, 16), 16)
            weights = w[pl.ds(i * GROUP + j, 2)].reshape(2 * ncells, columns)
            flux = jnp.dot(emitted[at, :], weights, preferred_element_type=F32)
            for s in range(2):
                at = pl.ds(i * GROUP + j + s, nbins, stride=nblocks)
                part[0, at, :] = flux[s * nbins:(s + 1) * nbins, 0:half]
                part[1, at, :] = flux[s * nbins:(s + 1) * nbins, half:columns]

    erode(0)
    emit(0)
    erode(1)

    def steps(i, carry):
        chunk(i - 2).wait()
        regrid(i - 2)
        emit(i - 1)
        erode(i)
        return carry

    middle = (groups + 2) // 2
    lax.fori_loop(2, middle, steps, 0)

    pl.semaphore_wait(barrier, n - 1)

    def send_surface(p):
        pltpu.make_async_remote_copy(
            src_ref=mine, dst_ref=gath.at[me], send_sem=surf_send, recv_sem=surf_recv,
            device_id=p, device_id_type=FLAT,
        ).start()

    each_peer(send_surface)
    gath[me] = mine[...]
    lax.fori_loop(middle, groups, steps, 0)
    chunk(groups - 2).wait()
    chunk(groups - 1).wait()
    regrid(groups - 2)
    emit(groups - 1)
    regrid(groups - 1)

    tiles = lax.broadcasted_iota(jnp.int32, (n, nblocks), 0)
    placing = jnp.where(jnp.broadcast_to(dest_v[...], (n, nblocks)) == tiles, 1.0, 0.0).astype(BF16)
    placing = jnp.concatenate([placing, placing], axis=1)
    for k in range(nbins):
        at = slice(k * nblocks, (k + 1) * nblocks)
        block = jnp.concatenate([part[0, at, :], part[1, at, :]], axis=1)
        high = block.astype(BF16)
        low = (block - high.astype(F32)).astype(BF16)
        total = jnp.dot(placing, jnp.concatenate([high, low], axis=0), preferred_element_type=F32)
        sums[pl.ds(k, n, stride=2 * nbins), :] = total[:, 0:half]
        sums[pl.ds(nbins + k, n, stride=2 * nbins), :] = total[:, half:columns]
    send[...] = sums[...].reshape(n, 2 * nbins, half).astype(BF16)

    def send_flux(p):
        pltpu.make_async_remote_copy(
            src_ref=send.at[p], dst_ref=came.at[me], send_sem=flux_send, recv_sem=flux_recv,
            device_id=p, device_id_type=FLAT,
        ).start()

    each_peer(send_flux)
    came[me] = send[me]

    for copy in copies[10:]:
        copy.wait()
    sink = rows_of([settle[0, f] for f in range(nbins)], (nbins, columns))
    ratios = [None] * levels
    values = [None] * levels
    for level in range(levels - 1, -1, -1):
        pivot = jnp.ones((nbins, columns), F32)
        at = pl.ds(level, nbins, stride=levels)
        right = jnp.concatenate([dust[0, at, :], dust[1, at, :]], axis=1)
        low = None
        if level > 0:
            low = jnp.broadcast_to(mix[level - 1:level, :], (nbins, columns))
            pivot = pivot + low
        if level < levels - 1:
            up = jnp.broadcast_to(mix[level:level + 1, :], (nbins, columns)) + sink
            pivot = pivot + up * (1.0 - ratios[level + 1])
            right = right + up * values[level + 1]
        else:
            pivot = pivot + sink
        inverse = 1.0 / pivot
        values[level] = right * inverse
        if low is not None:
            ratios[level] = low * inverse
    scale = float(columns) / float(ncells * nblocks)
    now, step = values[0], inverse * scale
    base[0], gain[0] = now, step
    for level in range(1, levels):
        now = values[level] + ratios[level] * now
        step = ratios[level] * step
        base[level], gain[level] = now, step

    arrived = gath.at[pl.ds(0, n - 1)]
    pltpu.make_async_copy(arrived, arrived, surf_recv).wait()
    rest = jnp.where(lax.broadcasted_iota(jnp.int32, (6, columns), 0) == 0, 1.0, 0.0)

    def back(i, carry):
        for j in range(0, GROUP, 2):
            g = i * GROUP + j
            left = jnp.concatenate(
                [gath[dest_s[0, g]], rest, gath[dest_s[0, g + 1]], rest], axis=0
            ).astype(BF16)
            weights = w[pl.ds(g, 2)].reshape(2 * ncells, columns)
            found = lax.dot_general(
                left, weights, (((1,), (1,)), ((), ())), preferred_element_type=F32
            )
            numer[pl.ds(pl.multiple_of(g * 8, 8), 8), :] = found[0:8, 0:ncells]
            numer[pl.ds(pl.multiple_of(g * 8 + 8, 8), 8), :] = found[8:16, ncells:2 * ncells]
        return carry

    lax.fori_loop(0, groups, back, 0)
    weight = 1.0 / numer[pl.ds(2, nblocks, stride=8), :]
    results[0:nblocks, :] = numer[pl.ds(0, nblocks, stride=8), :] * weight
    results[nblocks:2 * nblocks, :] = 0.5 * moist[...] + 0.5 * (numer[pl.ds(1, nblocks, stride=8), :] * weight)

    landed = came.at[pl.ds(0, n - 1)]
    pltpu.make_async_copy(landed, landed, flux_recv).wait()
    flux = jnp.sum(came[...].astype(F32), axis=0)
    flux = jnp.concatenate([flux[0:nbins], flux[nbins:2 * nbins]], axis=1)
    for level in range(levels):
        total = base[level] + gain[level] * flux
        for h in range(2):
            first = 2 * nblocks + h * nbins * levels + level
            results[pl.ds(first, nbins, stride=levels), :] = total[:, h * half:(h + 1) * half]

    sent = gath.at[pl.ds(0, n - 1)]
    pltpu.make_async_copy(sent, sent, surf_send).wait()
    gone = came.at[pl.ds(0, n - 1)]
    pltpu.make_async_copy(gone, gone, flux_send).wait()


def unpack(nblocks, half, results, land_out, dust_out, sem):
    rows = dust_out.shape[0]
    copies = [
        pltpu.make_async_copy(results.at[pl.ds(0, 2 * nblocks)], land_out, sem.at[0]),
        pltpu.make_async_copy(
            results.at[pl.ds(2 * nblocks, rows)], dust_out.at[:, 0:half], sem.at[1]
        ),
        pltpu.make_async_copy(
            results.at[pl.ds(2 * nblocks + rows, rows)], dust_out.at[:, half:2 * half], sem.at[2]
        ),
    ]
    for copy in copies:
        copy.start()
    for copy in copies:
        copy.wait()


def on_device(
    nt, land_wind, land_moist, texture, land_index, erod_map, mass_frac, blast_table, dest_tile,
    regrid_w, atm_state, dust_mix, mixing, settle,
):
    nblocks, ncells = land_wind.shape
    columns = regrid_w.shape[2]
    ntex, nbins, nsalt = blast_table.shape
    levels = atm_state.shape[1]
    half = columns // 2
    n = lax.axis_size(("sec", "tile"))
    groups = nblocks // GROUP
    soil = erod_map.reshape(-1, 128)
    operands = (
        land_wind, land_moist, texture, land_index, soil, mass_frac, blast_table,
        dest_tile.reshape(1, nblocks), regrid_w, atm_state,
        dust_mix.reshape(nbins * levels, columns), mixing, settle.reshape(1, nbins),
    )
    land = pltpu.VMEM((nblocks, ncells), F32)
    whole = pltpu.VMEM((nblocks, ncells), jnp.int32)
    results = pl.pallas_call(
        functools.partial(kernel, n, nt, nblocks, ncells, columns, nbins, nsalt, ntex, levels),
        out_shape=jax.ShapeDtypeStruct((2 * nblocks + 2 * nbins * levels, 128), F32),
        in_specs=[pl.BlockSpec(memory_space=pltpu.HBM)] * 13,
        out_specs=pl.BlockSpec(memory_space=pltpu.VMEM),
        scratch_shapes=[
            land,
            land,
            whole,
            whole,
            pltpu.VMEM(soil.shape, F32),
            pltpu.VMEM(mass_frac.shape, F32),
            pltpu.VMEM(blast_table.shape, F32),
            pltpu.VMEM((1, nblocks), jnp.int32),
            pltpu.SMEM((1, nblocks), jnp.int32),
            pltpu.VMEM(regrid_w.shape, BF16),
            pltpu.VMEM(atm_state.shape, F32),
            pltpu.VMEM((2, nbins * levels, half), F32),
            pltpu.VMEM(mixing.shape, F32),
            pltpu.SMEM((1, nbins), F32),
            pltpu.VMEM((soil.shape[0] // 2, 128), jnp.int32),
            land,
            land,
            pltpu.VMEM((nbins, 128), F32),
            pltpu.VMEM((nblocks * nbins, columns), BF16),
            pltpu.VMEM((2, nbins * nblocks, half), F32),
            pltpu.VMEM((n * 2 * nbins, half), F32),
            pltpu.VMEM((n, 2 * nbins, half), BF16),
            pltpu.VMEM((n, 2 * nbins, half), BF16),
            pltpu.VMEM((2, columns), F32),
            pltpu.VMEM((n, 2, columns), F32),
            pltpu.VMEM((nblocks * 8, ncells), F32),
            pltpu.VMEM((levels, nbins, columns), F32),
            pltpu.VMEM((levels, nbins, columns), F32),
            pltpu.SemaphoreType.DMA((14,)),
            pltpu.SemaphoreType.DMA((groups,)),
            pltpu.SemaphoreType.DMA,
            pltpu.SemaphoreType.DMA,
            pltpu.SemaphoreType.DMA,
            pltpu.SemaphoreType.DMA,
        ],
        compiler_params=pltpu.CompilerParams(
            collective_id=0, has_side_effects=True, vmem_limit_bytes=40 * 1024 * 1024
        ),
    )(*(pltpu.with_memory_space_constraint(x, pltpu.HBM) for x in operands))
    land_out, dust_out = pl.pallas_call(
        functools.partial(unpack, nblocks, half),
        out_shape=(
            jax.ShapeDtypeStruct((2 * nblocks, ncells), F32),
            jax.ShapeDtypeStruct((nbins * levels, columns), F32),
        ),
        in_specs=[pl.BlockSpec(memory_space=pltpu.VMEM)],
        out_specs=(pl.BlockSpec(memory_space=pltpu.HBM), pl.BlockSpec(memory_space=pltpu.HBM)),
        scratch_shapes=[pltpu.SemaphoreType.DMA((3,))],
        compiler_params=pltpu.CompilerParams(vmem_limit_bytes=16 * 1024 * 1024),
    )(pltpu.with_memory_space_constraint(results, pltpu.VMEM))
    return land_out.reshape(2, nblocks, ncells), dust_out.reshape(nbins, levels, columns)


def solution(mesh):
    both = ("sec", "tile")
    in_specs = (
        P(both, None),
        P(both, None),
        P(both, None),
        P(both, None),
        P(both),
        P(),
        P(),
        P(both, None),
        P(both, None, None),
        P(None, None, both),
        P(None, None, both),
        P(None, both),
        P(),
    )
    out_specs = (P(None, both, None), P(None, None, both))
    return jax.shard_map(
        functools.partial(on_device, mesh.shape["tile"]),
        mesh=mesh, in_specs=in_specs, out_specs=out_specs, check_vma=False,
    )
```
